32 devices in a mesh: parts: 2 (over y), expert: 4 (over z), tensor: 4 (over x, core).
Axes of the slice: x: 2, y: 2, z: 4, core: 2. Of those that a mesh axis runs over, the one named last changes fastest.
Arguments:
- tokens_in: bfloat16 [512, 3072], P(('parts', 'expert', 'tensor')), parts along dimension 0, may hold values from -6 to 6
- out_grad: bfloat16 [512, 3072], P(('parts', 'expert', 'tensor')), parts along dimension 0, may hold values from -6 to 6
- expert_ids: int32 [512, 2], P(('parts', 'expert', 'tensor')), parts along dimension 0, may hold values from 0 to 3, all different within a row; in each aligned block of 64 rows (0 to 63, 64 to 127, ...) at most 48 rows name the same one
- gate_probs: bfloat16 [512, 2], P(('parts', 'expert', 'tensor')), parts along dimension 0, may hold values from 0.099609375 to 1
- w_in: bfloat16 [4, 3072, 8192], P('expert', None, 'tensor'), may hold values from -0.109375 to 0.109375
- w_out: bfloat16 [4, 8192, 3072], P('expert', 'tensor'), may hold values from -0.0625 to 0.0625
Outputs:
- token_grad: bfloat16 [512, 3072], P(('parts', 'expert', 'tensor')), parts along dimension 0
The draws below stay inside these ranges and needn't reach their ends.
There are 2 independent parts, one for each index of `parts`. The reference program is written for one: setup_inputs(seed, part) draws one part's arguments, and reference() takes and returns one part's arrays. A program takes and returns all parts, laid end to end along the dimension named above; an argument that names none is the same for every part. Nothing has to cross between parts.
Inputs may be any that keep to these rules, and one draw needn't show every extreme that they name: `expert_ids`: each token names two different experts. In each aligned block of 64 tokens no expert is named by more than 48 tokens, a bound that some block reaches.
All inputs are finite; a program needn't handle non-finite values.
Results may differ from the reference program's by a relative error of at most 0.02.
Values may be sent and summed in bfloat16 or wider, within the bound.
No kernel may reach another device: no remote copies, remote signals or barrier semaphores. Data moves between devices by JAX's collectives and lax.ppermute only.
A program may use at most 64 MiB of HBM per device.

```python
import math
import jax
import jax.numpy as jnp
import numpy as np
from jax import lax

D = 3072
H = 8192
EXPERTS = 4
GROUP_TOK = 64
TOKENS = 256
CAP = 48
N_TENSOR = 4


def shard_levels(stream_key, dims, split, smallest, high):
    loudness = 1.0
    for position, shards_of in split:
        heights = jax.random.uniform(jax.random.fold_in(jax.random.fold_in(stream_key, 6), position), (shards_of,), jnp.float32, smallest / len(split), high / len(split))
        loudness = loudness * jnp.repeat(jnp.exp(heights), dims[position] // shards_of).reshape((-1,) + (1,) * (len(dims) - 1 - position))
    return loudness


def routed_block(stream_key, own, number, rows, count, top, reach, slope):
    sequence = jax.random.permutation(stream_key, count)
    crowded, ordinary = shares(count, rows * top, reach, slope, True), shares(count, rows * top, reach, slope, False)
    places = jnp.arange(count)

    def named(lengths, rotation):
        used = int((lengths > 0).sum())
        fixed = max(1, used // 4)
        passed = fixed + (places - fixed + rotation * (used - fixed)) % max(1, count - fixed)
        return jnp.zeros((count,), jnp.int32).at[sequence[jnp.where(places < fixed, places, passed)]].set(jnp.asarray(lengths, jnp.int32))

    lengths = jnp.where(number % 4 == 0, named(crowded, number // 4), named(ordinary, number - number // 4 - 1))
    mixed = jax.random.permutation(jax.random.fold_in(own, 3), count)
    donor, sink = mixed[0:count // 2 * 2:2], mixed[1:count // 2 * 2:2]
    slack = jnp.minimum(lengths[donor] - 1, reach - lengths[sink]) // 2
    slack = jnp.where((donor == sequence[0]) | (sink == sequence[0]) | (lengths[sink] == 0), 0, jnp.maximum(slack, 0))
    passed = jax.random.randint(jax.random.fold_in(own, 4), (count // 2,), 0, 1 << 20) % (slack + 1)
    lengths = lengths.at[donor].add(-passed).at[sink].add(passed)
    items = jnp.searchsorted(jnp.cumsum(lengths), jnp.arange(rows * top), side="right").astype(jnp.int32)
    listing = items.reshape(top, rows).T
    listing = listing[jax.random.permutation(jax.random.fold_in(own, 1), rows)]
    rotation = jax.random.randint(jax.random.fold_in(own, 2), (rows, 1), 0, top)
    return jnp.take_along_axis(listing, (jnp.arange(top)[None, :] + rotation) % top, axis=1)


def shares(amount, total, limit, slope, full):
    weights = [(1 << 20) // math.isqrt(grade ** slope) + 1 for grade in range(1, amount + 1)]
    largest = limit if full else min(limit, max(-(-total // amount), total * weights[0] // sum(weights)))
    least = 1 if total - largest >= amount - 1 else 0
    counts, spare = [largest] + [least] * (amount - 1), total - largest - least * (amount - 1)
    while spare > 0:
        movable = [i for i in range(1, amount) if counts[i] < largest] or [i for i in range(1, amount) if counts[i] < limit]
        whole, budget = sum([weights[i] for i in movable]), spare
        for i in movable:
            addition = min(limit - counts[i], max(1, budget * weights[i] // whole), spare)
            counts[i] = counts[i] + addition
            spare = spare - addition
    return np.array(counts)


def bell_draw(own_key, extent, spread, most, pieces=(), kind=jnp.bfloat16):
    result = jax.random.normal(own_key, extent, jnp.float32) * spread
    if len(pieces) > 0:
        result = shard_levels(own_key, extent, pieces, -0.22, 0.18) * result
    return jnp.clip(result, min=-most, max=most).astype(kind)


def setup_inputs(seed: int = 0, part: int = 0) -> dict:
    keys = jax.random.split(jax.random.key(seed), 7)
    part_keys = jax.random.split(jax.random.fold_in(keys[6], part), 7)
    tokens_in = bell_draw(part_keys[0], (TOKENS, D), 1.0, 6.0, ((0, 16),))
    out_grad = bell_draw(part_keys[1], (TOKENS, D), 1.0, 6.0, ((0, 16),))
    expert_ids_keys = jax.random.split(jax.random.fold_in(part_keys[2], 1), TOKENS // GROUP_TOK)
    expert_ids_turns = jax.random.permutation(jax.random.fold_in(part_keys[2], 3), TOKENS // GROUP_TOK)
    expert_ids = jax.vmap(lambda own, number: routed_block(jax.random.fold_in(part_keys[2], 2), own, number, GROUP_TOK, EXPERTS, 2, CAP, 2))(expert_ids_keys, expert_ids_turns).reshape((TOKENS, 2))
    gate_probs = jnp.clip(0.099609375 + 0.9003906 * jax.random.uniform(part_keys[3], (TOKENS, 2), jnp.float32) ** shard_levels(part_keys[3], (TOKENS, 2), ((0, 16),), -0.2, 0.2), 0.099609375, 1.0).astype(jnp.bfloat16)
    w_in = bell_draw(keys[4], (EXPERTS, D, H), D ** -0.5, 0.109375, ((0, 4), (2, 4)))
    w_out = bell_draw(keys[5], (EXPERTS, H, D), H ** -0.5, 0.0625, ((0, 4), (1, 4)))
    return dict(tokens_in=tokens_in, out_grad=out_grad, expert_ids=expert_ids, gate_probs=gate_probs, w_in=w_in, w_out=w_out)


def gelu_slope(value):
    coeff = math.sqrt(2.0 / math.pi)
    inner = jnp.tanh(coeff * (value + 0.044715 * value * value * value))
    return 0.5 * (1.0 + inner) + 0.5 * value * (1.0 - inner * inner) * coeff * (1.0 + 3.0 * 0.044715 * value * value)

def reference(tokens_in, out_grad, expert_ids, gate_probs, w_in, w_out):
    flat_ids = expert_ids.reshape(-1).astype(jnp.int32)
    pair_count = flat_ids.shape[0]
    per_expert = EXPERTS * CAP
    run_width = H // N_TENSOR
    flat_gates = gate_probs.reshape(-1)

    def one_expert(expert):
        chosen = flat_ids == expert
        rank_in = jnp.cumsum(chosen.astype(jnp.int32)) - 1
        place = jnp.where(chosen, rank_in, per_expert).astype(jnp.int32)
        source = jnp.zeros((per_expert + 1,), jnp.int32).at[place].set(jnp.arange(pair_count, dtype=jnp.int32))[:per_expert]
        valid = jnp.zeros((per_expert + 1,), jnp.float32).at[place].set(1.0)[:per_expert]
        token_of = (source // 2).astype(jnp.int32)
        rows_in = tokens_in[token_of].astype(jnp.float32) * valid[:, None]
        rows_grad = out_grad[token_of].astype(jnp.float32) * valid[:, None]
        rows_gate = flat_gates[source].astype(jnp.float32) * valid
        weight_in = w_in[expert].astype(jnp.float32)
        weight_out = w_out[expert].astype(jnp.float32)
        preact = jnp.dot(rows_in, weight_in, precision=lax.Precision.HIGHEST)
        hidden_grad = jnp.dot(rows_grad, weight_out.T, precision=lax.Precision.HIGHEST)
        scaled = rows_gate[:, None] * hidden_grad * gelu_slope(preact)
        scaled = lax.optimization_barrier(scaled.astype(jnp.bfloat16)).astype(jnp.float32)
        scaled_runs = scaled.reshape(per_expert, N_TENSOR, run_width)
        weight_runs = weight_in.reshape(D, N_TENSOR, run_width)
        partial_rows = jnp.einsum('rsh,dsh->srd', scaled_runs, weight_runs, precision=lax.Precision.HIGHEST)
        partial_rows = lax.optimization_barrier(partial_rows.astype(jnp.bfloat16)).astype(jnp.float32)
        summed = lax.optimization_barrier(jnp.sum(partial_rows, axis=0)).astype(jnp.bfloat16)
        return (summed, source, valid)
    results, sources, valids = lax.map(one_expert, jnp.arange(EXPERTS, dtype=jnp.int32))
    where_to = jnp.where(valids > 0.5, sources, pair_count).astype(jnp.int32).reshape(-1)
    pair_rows = jnp.zeros((pair_count + 1, D), jnp.float32).at[where_to].add(results.reshape(-1, D).astype(jnp.float32))
    pair_rows = pair_rows[:pair_count].reshape(TOKENS, 2, D)
    return lax.optimization_barrier(jnp.sum(pair_rows, axis=1)).astype(jnp.bfloat16)
```

```python
import math

import jax
import jax.numpy as jnp
from jax import lax
from jax.experimental import pallas as pl
from jax.experimental.pallas import tpu as pltpu
from jax.sharding import PartitionSpec as P


def gelu_slope(value):
    coeff = math.sqrt(2.0 / math.pi)
    inner = jnp.tanh(coeff * (value + 0.044715 * value * value * value))
    return 0.5 * (1.0 + inner) + 0.5 * value * (1.0 - inner * inner) * coeff * (
        1.0 + 3.0 * 0.044715 * value * value
    )


def slot_table(route_all, experts, capacity):
    flat_ids = route_all.reshape(-1)
    pair_count = flat_ids.shape[0]
    onehot = (flat_ids[:, None] == jnp.arange(experts, dtype=jnp.int32)[None, :]).astype(jnp.int32)
    before = jnp.cumsum(onehot, axis=0) - onehot
    slot_index = jnp.sum(before * onehot, axis=1)
    target = flat_ids * capacity + slot_index
    cell_index = jnp.arange(experts * capacity, dtype=jnp.int32)
    matches = target[None, :] == cell_index[:, None]
    source = jnp.sum(
        jnp.where(matches, jnp.arange(pair_count, dtype=jnp.int32)[None, :], 0), axis=1
    )
    filled = jnp.any(matches, axis=1)
    return (target, source, filled)


def routed(tokens_in, out_grad, expert_ids, gate_probs, w_in, w_out):
    experts = lax.axis_size("expert")
    shards = lax.axis_size("tensor")
    local_rows = tokens_in.shape[0]
    features = tokens_in.shape[1]
    capacity = 3 * local_rows * shards // experts
    route_all = lax.all_gather(expert_ids, "tensor", axis=0, tiled=True)
    target, source, filled = slot_table(route_all, experts, capacity)
    inputs_all, grads_all, gates_all = (
        lax.all_gather(tokens_in, "tensor", axis=0, tiled=True),
        lax.all_gather(out_grad, "tensor", axis=0, tiled=True),
        lax.all_gather(gate_probs, "tensor", axis=0, tiled=True),
    )
    token_of = source // 2
    occupied = filled[:, None]
    send_in = jnp.where(occupied, jnp.take(inputs_all, token_of, axis=0), 0)
    send_in = send_in.reshape(experts, capacity, -1)
    send_grad = jnp.where(occupied, jnp.take(grads_all, token_of, axis=0), 0)
    send_grad = send_grad.reshape(experts, capacity, -1)
    send_gate = jnp.where(filled, jnp.take(gates_all.reshape(-1), source), 0)
    send_gate = send_gate.reshape(experts, capacity)
    rows_in = lax.all_to_all(send_in, "expert", split_axis=0, concat_axis=0, tiled=True)
    rows_grad = lax.all_to_all(send_grad, "expert", split_axis=0, concat_axis=0, tiled=True)
    rows_gate = lax.all_to_all(send_gate, "expert", split_axis=0, concat_axis=0, tiled=True)
    slot_count = rows_in.shape[1]
    flat_in = rows_in.reshape(-1, features)
    flat_grad = rows_grad.reshape(-1, features)
    preact = jnp.dot(flat_in, w_in[0], preferred_element_type=jnp.float32)
    hidden_grad = jnp.einsum("rd,hd->rh", flat_grad, w_out[0], preferred_element_type=jnp.float32)
    scaled = (
        rows_gate.reshape(-1, 1).astype(jnp.float32) * hidden_grad * gelu_slope(preact)
    ).astype(jnp.bfloat16)
    partial_rows = jnp.einsum(
        "rh,dh->rd", scaled, w_in[0], preferred_element_type=jnp.float32
    ).astype(jnp.bfloat16)
    summed = lax.psum(partial_rows, "tensor").astype(jnp.float32)
    outgoing = summed.astype(jnp.bfloat16).reshape(experts, slot_count, -1)
    returned = lax.all_to_all(outgoing, "expert", split_axis=0, concat_axis=0, tiled=True)
    row_table = returned.reshape(experts * capacity, -1)
    offset_row = lax.axis_index("tensor") * (2 * local_rows)
    own_rows = lax.dynamic_slice_in_dim(target, offset_row, 2 * local_rows)
    picked = (
        jnp.take(row_table, own_rows, axis=0).astype(jnp.float32).reshape(local_rows, 2, features)
    )
    return jnp.sum(picked, axis=1).astype(jnp.bfloat16)


CORES = 2
LANES = 128
CHUNKS = 2
NT = (((1,), (1,)), ((), ()))


def in_vmem(array):
    return pltpu.with_memory_space_constraint(array, pltpu.VMEM)


def whole_block():
    return pl.BlockSpec(memory_space=pltpu.VMEM)


def assemble(pieces, rows_ref):
    start = 0
    width = rows_ref.shape[1]
    for piece in pieces:
        rows_ref[pl.ds(start, piece.shape[0]), :] = piece[:, :width]
        start += piece.shape[0]


def slope_rows(pieces, weight, tile):
    rows = sum(piece.shape[0] for piece in pieces)
    features, width = weight.shape

    def kernel(*refs):
        *piece_refs, weight_ref, out_ref, rows_ref = refs
        assemble(piece_refs, rows_ref)

        @pl.loop(0, width // tile)
        def _(step):
            cols = pl.ds(pl.multiple_of(step * tile, tile), tile)
            preact = jnp.dot(
                rows_ref[...], weight_ref[:, cols], preferred_element_type=jnp.float32
            )
            out_ref[:, cols] = gelu_slope(preact)

    return pl.pallas_call(
        kernel,
        out_shape=jax.ShapeDtypeStruct((rows, width), jnp.float32),
        in_specs=[whole_block()] * (len(pieces) + 1),
        out_specs=whole_block(),
        scratch_shapes=[pltpu.VMEM((rows, features), jnp.bfloat16)],
        compiler_params=pltpu.CompilerParams(vmem_limit_bytes=16 * 2**20),
        cost_estimate=pl.CostEstimate(
            flops=2 * rows * features * width,
            bytes_accessed=4 * rows * width + 2 * rows * features,
            transcendentals=rows * width,
        ),
    )(*pieces, in_vmem(weight))


def scaled_rows(pieces, weight, slope, tile):
    rows, width = slope.shape
    features = weight.shape[1]

    def kernel(expert_ref, *refs):
        *piece_refs, weight_ref, slope_ref, out_ref, rows_ref, gate_ref = refs
        assemble(piece_refs, rows_ref)
        start = 0
        for piece in piece_refs:
            gates = piece[:, features:].astype(jnp.float32)
            lane = lax.broadcasted_iota(jnp.int32, gates.shape, 1)
            gate_ref[pl.ds(start, piece.shape[0]), :] = jnp.sum(
                jnp.where(lane == expert_ref[0], gates, 0.0), axis=1, keepdims=True
            )
            start += piece.shape[0]

        @pl.loop(0, width // tile)
        def _(step):
            cols = pl.ds(pl.multiple_of(step * tile, tile), tile)
            hidden_grad = lax.dot_general(
                rows_ref[...], weight_ref[cols, :], NT, preferred_element_type=jnp.float32
            )
            out_ref[:, cols] = (gate_ref[...] * hidden_grad * slope_ref[:, cols]).astype(
                jnp.bfloat16
            )

    expert = lax.axis_index("expert").astype(jnp.int32).reshape(1)
    return pl.pallas_call(
        kernel,
        out_shape=jax.ShapeDtypeStruct((rows, width), jnp.bfloat16),
        in_specs=[pl.BlockSpec(memory_space=pltpu.SMEM)] + [whole_block()] * (len(pieces) + 2),
        out_specs=whole_block(),
        scratch_shapes=[
            pltpu.VMEM((rows, features), jnp.bfloat16),
            pltpu.VMEM((rows, 1), jnp.float32),
        ],
        compiler_params=pltpu.CompilerParams(vmem_limit_bytes=16 * 2**20),
        cost_estimate=pl.CostEstimate(
            flops=2 * rows * features * width,
            bytes_accessed=6 * rows * width + 2 * rows * features,
            transcendentals=0,
        ),
    )(expert, *pieces, in_vmem(weight), slope)


def partial_rows(scaled, weight, first, count, tile):
    rows, width = scaled.shape
    half = rows // CORES

    def kernel(scaled_ref, weight_ref, *out_refs):
        @pl.loop(0, count // tile)
        def _(step):
            offset = pl.multiple_of(step * tile, tile)
            cols = pl.ds(offset, tile)
            product = lax.dot_general(
                scaled_ref[...],
                weight_ref[pl.ds(first + offset, tile), :],
                NT,
                preferred_element_type=jnp.float32,
            ).astype(jnp.bfloat16)
            for place, out_ref in enumerate(out_refs):
                out_ref[:, cols] = product[place * half : (place + 1) * half]

    return pl.pallas_call(
        kernel,
        out_shape=[jax.ShapeDtypeStruct((half, count), jnp.bfloat16)] * CORES,
        in_specs=[whole_block()] * 2,
        out_specs=[whole_block()] * CORES,
        compiler_params=pltpu.CompilerParams(vmem_limit_bytes=16 * 2**20),
        cost_estimate=pl.CostEstimate(
            flops=2 * rows * count * width,
            bytes_accessed=2 * rows * (count + width),
            transcendentals=0,
        ),
    )(scaled, in_vmem(weight))


def along_expert(array, shift):
    size = lax.axis_size("expert")
    return lax.ppermute(array, "expert", [(i, (i + shift) % size) for i in range(size)])


def along_chips(array, shift):
    size = lax.axis_size("tensor")
    return lax.ppermute(
        array, "tensor", [(i, (i + CORES * shift) % size) for i in range(size)]
    )


def other_core(array):
    size = lax.axis_size("tensor")
    return lax.ppermute(array, "tensor", [(i, i ^ 1) for i in range(size)])


def gather_rows(block):
    experts, chips = lax.axis_size("expert"), lax.axis_size("tensor") // CORES
    rows = block.shape[0]
    column = jnp.concatenate(
        [block] + [along_expert(block, shift) for shift in range(1, experts)], axis=0
    )
    pieces = [column]
    for shift in range(1, chips):
        pieces.append(along_chips(block, shift))
        pieces.append(along_chips(column[rows:], shift))
    beside = jnp.concatenate(pieces[1:], axis=0)
    return [column, beside, other_core(column), other_core(beside)]


def add_rows(*terms):
    total = terms[0].astype(jnp.float32)
    for term in terms[1:]:
        total = total + term.astype(jnp.float32)
    return total.astype(jnp.bfloat16)


def scatter_rows(kept, sent, rows):
    experts, chips = lax.axis_size("expert"), lax.axis_size("tensor") // CORES
    total = add_rows(kept, other_core(sent))
    column = rows * experts
    total = add_rows(
        total[:column],
        *[
            along_chips(total[shift * column : (shift + 1) * column], -shift)
            for shift in range(1, chips)
        ],
    )
    return add_rows(
        total[:rows],
        *[
            along_expert(total[shift * rows : (shift + 1) * rows], -shift)
            for shift in range(1, experts)
        ],
    )


def dense(tokens_in, out_grad, expert_ids, gate_probs, w_in, w_out):
    local_rows, features = tokens_in.shape
    lane = jnp.arange(LANES, dtype=jnp.int32)
    named = expert_ids[:, :, None] == lane
    gates = jnp.sum(jnp.where(named, gate_probs[:, :, None].astype(jnp.float32), 0.0), axis=1)
    grads = jnp.concatenate([out_grad, gates.astype(jnp.bfloat16)], axis=1)
    input_pieces = gather_rows(tokens_in)
    grad_pieces = gather_rows(grads)
    slope = slope_rows(input_pieces, w_in[0], 1024)
    scaled = scaled_rows(grad_pieces, w_out[0], slope, 1024)
    count = features // CHUNKS
    chunks = [
        scatter_rows(*partial_rows(scaled, w_in[0], place * count, count, 768), local_rows)
        for place in range(CHUNKS)
    ]
    return jnp.concatenate(chunks, axis=1)


def local(*args):
    experts = lax.axis_size("expert")
    if experts <= 6 and lax.axis_size("tensor") % CORES == 0:
        return dense(*args)
    return routed(*args)


def solution(mesh):
    return jax.shard_map(
        local,
        mesh=mesh,
        in_specs=(
            P(("parts", "expert", "tensor"), None),
            P(("parts", "expert", "tensor"), None),
            P(("parts", "expert", "tensor"), None),
            P(("parts", "expert", "tensor"), None),
            P("expert", None, "tensor"),
            P("expert", "tensor", None),
        ),
        out_specs=P(("parts", "expert", "tensor"), None),
        check_vma=False,
    )
```

```python
import math

import jax
import jax.numpy as jnp
from jax import lax
from jax.experimental import pallas as pl
from jax.experimental.pallas import tpu as pltpu
from jax.sharding import PartitionSpec as P


def gelu_slope(value):
    coeff = math.sqrt(2.0 / math.pi)
    inner = jnp.tanh(coeff * (value + 0.044715 * value * value * value))
    return 0.5 * (1.0 + inner) + 0.5 * value * (1.0 - inner * inner) * coeff * (
        1.0 + 3.0 * 0.044715 * value * value
    )


def slot_table(route_all, experts, capacity):
    flat_ids = route_all.reshape(-1)
    pair_count = flat_ids.shape[0]
    onehot = (flat_ids[:, None] == jnp.arange(experts, dtype=jnp.int32)[None, :]).astype(jnp.int32)
    before = jnp.cumsum(onehot, axis=0) - onehot
    slot_index = jnp.sum(before * onehot, axis=1)
    target = flat_ids * capacity + slot_index
    cell_index = jnp.arange(experts * capacity, dtype=jnp.int32)
    matches = target[None, :] == cell_index[:, None]
    source = jnp.sum(
        jnp.where(matches, jnp.arange(pair_count, dtype=jnp.int32)[None, :], 0), axis=1
    )
    filled = jnp.any(matches, axis=1)
    return (target, source, filled)


def routed(tokens_in, out_grad, expert_ids, gate_probs, w_in, w_out):
    experts = lax.axis_size("expert")
    shards = lax.axis_size("tensor")
    local_rows = tokens_in.shape[0]
    features = tokens_in.shape[1]
    capacity = 3 * local_rows * shards // experts
    route_all = lax.all_gather(expert_ids, "tensor", axis=0, tiled=True)
    target, source, filled = slot_table(route_all, experts, capacity)
    inputs_all, grads_all, gates_all = (
        lax.all_gather(tokens_in, "tensor", axis=0, tiled=True),
        lax.all_gather(out_grad, "tensor", axis=0, tiled=True),
        lax.all_gather(gate_probs, "tensor", axis=0, tiled=True),
    )
    token_of = source // 2
    occupied = filled[:, None]
    send_in = jnp.where(occupied, jnp.take(inputs_all, token_of, axis=0), 0)
    send_in = send_in.reshape(experts, capacity, -1)
    send_grad = jnp.where(occupied, jnp.take(grads_all, token_of, axis=0), 0)
    send_grad = send_grad.reshape(experts, capacity, -1)
    send_gate = jnp.where(filled, jnp.take(gates_all.reshape(-1), source), 0)
    send_gate = send_gate.reshape(experts, capacity)
    rows_in = lax.all_to_all(send_in, "expert", split_axis=0, concat_axis=0, tiled=True)
    rows_grad = lax.all_to_all(send_grad, "expert", split_axis=0, concat_axis=0, tiled=True)
    rows_gate = lax.all_to_all(send_gate, "expert", split_axis=0, concat_axis=0, tiled=True)
    slot_count = rows_in.shape[1]
    flat_in = rows_in.reshape(-1, features)
    flat_grad = rows_grad.reshape(-1, features)
    preact = jnp.dot(flat_in, w_in[0], preferred_element_type=jnp.float32)
    hidden_grad = jnp.einsum("rd,hd->rh", flat_grad, w_out[0], preferred_element_type=jnp.float32)
    scaled = (
        rows_gate.reshape(-1, 1).astype(jnp.float32) * hidden_grad * gelu_slope(preact)
    ).astype(jnp.bfloat16)
    partial_rows = jnp.einsum(
        "rh,dh->rd", scaled, w_in[0], preferred_element_type=jnp.float32
    ).astype(jnp.bfloat16)
    summed = lax.psum(partial_rows, "tensor").astype(jnp.float32)
    outgoing = summed.astype(jnp.bfloat16).reshape(experts, slot_count, -1)
    returned = lax.all_to_all(outgoing, "expert", split_axis=0, concat_axis=0, tiled=True)
    row_table = returned.reshape(experts * capacity, -1)
    offset_row = lax.axis_index("tensor") * (2 * local_rows)
    own_rows = lax.dynamic_slice_in_dim(target, offset_row, 2 * local_rows)
    picked = (
        jnp.take(row_table, own_rows, axis=0).astype(jnp.float32).reshape(local_rows, 2, features)
    )
    return jnp.sum(picked, axis=1).astype(jnp.bfloat16)


CORES = 2
EXPERTS = 4
NEAR, FAR = 1, (2, 3)
LANES = 128
NT = (((1,), (1,)), ((), ()))
VMEM_LIMIT = 24 * 2**20
NO_COST = pl.CostEstimate(flops=0, bytes_accessed=0, transcendentals=0)


def in_vmem(array):
    return pltpu.with_memory_space_constraint(array, pltpu.VMEM)


def whole_block():
    return pl.BlockSpec(memory_space=pltpu.VMEM)


def after(array, *earlier):
    return lax.optimization_barrier((array, *earlier))[0]


def assemble(pieces, rows_ref):
    start = 0
    for piece in pieces:
        rows_ref[pl.ds(start, piece.shape[0]), :] = piece[:, : rows_ref.shape[1]]
        start += piece.shape[0]


def small_kernel(kernel, out_shape, operands):
    return pl.pallas_call(
        kernel,
        out_shape=out_shape,
        in_specs=[whole_block()] * len(operands),
        out_specs=jax.tree.map(lambda _: whole_block(), out_shape),
        compiler_params=pltpu.CompilerParams(vmem_limit_bytes=VMEM_LIMIT),
        cost_estimate=NO_COST,
    )(*operands)


def stacked(*pieces, width=None, offsets=None):
    width = width or pieces[0].shape[1]
    offsets = offsets or [0] * len(pieces)
    rows = sum(piece.shape[0] for piece in pieces)

    def kernel(*refs):
        out_ref = refs[-1]
        start = 0
        for piece, offset in zip(refs, offsets):
            out_ref[pl.ds(start, piece.shape[0]), :] = piece[:, offset : offset + width]
            start += piece.shape[0]

    return small_kernel(kernel, jax.ShapeDtypeStruct((rows, width), jnp.bfloat16), pieces)


def added(terms, sizes):
    width = terms[0].shape[1]

    def kernel(*refs):
        term_refs, out_refs = refs[: len(terms)], refs[len(terms) :]
        start = 0
        for out_ref in out_refs:
            rows = pl.ds(start, out_ref.shape[0])
            total = term_refs[0][rows, :].astype(jnp.float32)
            for term_ref in term_refs[1:]:
                total += term_ref[rows, :].astype(jnp.float32)
            out_ref[...] = total.astype(jnp.bfloat16)
            start += out_ref.shape[0]

    return small_kernel(
        kernel, [jax.ShapeDtypeStruct((size, width), jnp.bfloat16) for size in sizes], terms
    )


def added_beside(chunks):
    rows = chunks[0][0].shape[0]
    widths = [chunk[0].shape[1] for chunk in chunks]
    terms = [term for chunk in chunks for term in chunk]

    def kernel(*refs):
        *term_refs, out_ref = refs
        start = 0
        for chunk, width in zip(chunks, widths):
            group, term_refs = term_refs[: len(chunk)], term_refs[len(chunk) :]
            total = group[0][...].astype(jnp.float32)
            for term_ref in group[1:]:
                total += term_ref[...].astype(jnp.float32)
            out_ref[:, start : start + width] = total.astype(jnp.bfloat16)
            start += width

    return small_kernel(kernel, jax.ShapeDtypeStruct((rows, sum(widths)), jnp.bfloat16), terms)


def in_hbm(array):
    return pltpu.with_memory_space_constraint(array, pltpu.HBM)


def hbm_block():
    return pl.BlockSpec(memory_space=pltpu.HBM)


def with_gates(tokens, grads, expert_ids, gate_probs):
    rows, features = grads.shape

    def kernel(tokens_ref, grads_ref, ids_ref, probs_ref, out_ref, both_ref, ids, probs, sems):
        copies = [
            pltpu.make_async_copy(source, target, sems.at[place])
            for place, (source, target) in enumerate(
                (
                    (ids_ref, ids),
                    (probs_ref, probs),
                    (tokens_ref, both_ref.at[:, pl.ds(0, features)]),
                    (grads_ref, both_ref.at[:, pl.ds(features, features)]),
                    (grads_ref, out_ref.at[:, pl.ds(0, features)]),
                )
            )
        ]
        for copy in copies:
            copy.start()
        copies[0].wait()
        copies[1].wait()
        lane = lax.broadcasted_iota(jnp.int32, (rows, LANES), 1)
        here = lax.broadcasted_iota(jnp.int32, (rows, rows), 0) == lax.broadcasted_iota(
            jnp.int32, (rows, rows), 1
        )
        upright = lambda row: jnp.sum(jnp.where(here, row, 0.0), axis=1, keepdims=True)
        gates = jnp.zeros((rows, LANES), jnp.float32)
        for k in range(ids.shape[0]):
            named = upright(ids[k : k + 1, :].astype(jnp.float32)).astype(jnp.int32)
            prob = upright(probs[k : k + 1, :].astype(jnp.float32))
            gates += jnp.where(lane == named, prob, 0.0)
        out_ref[:, features:] = gates.astype(jnp.bfloat16)
        both_ref[:, 2 * features :] = gates.astype(jnp.bfloat16)
        for copy in copies[2:]:
            copy.wait()

    return pl.pallas_call(
        kernel,
        out_shape=[
            jax.ShapeDtypeStruct((rows, features + LANES), jnp.bfloat16),
            jax.ShapeDtypeStruct((rows, 2 * features + LANES), jnp.bfloat16),
        ],
        in_specs=[hbm_block()] * 4,
        out_specs=[whole_block()] * 2,
        scratch_shapes=[
            pltpu.VMEM(expert_ids.shape[::-1], expert_ids.dtype),
            pltpu.VMEM(gate_probs.shape[::-1], gate_probs.dtype),
            pltpu.SemaphoreType.DMA((5,)),
        ],
        compiler_params=pltpu.CompilerParams(vmem_limit_bytes=VMEM_LIMIT),
        cost_estimate=NO_COST,
    )(in_hbm(tokens), in_hbm(grads), in_hbm(expert_ids.T), in_hbm(gate_probs.T))


def streamed(source_ref, target_ref, sems, first, parts, axis=0):
    size = target_ref.shape[axis] // parts
    copies = []
    for part in range(parts):
        here, there = pl.ds(first + part * size, size), pl.ds(part * size, size)
        if axis == 0:
            ends = source_ref.at[here], target_ref.at[there]
        else:
            ends = source_ref.at[:, here], target_ref.at[:, there]
        copies.append(pltpu.make_async_copy(*ends, sems.at[part]))
        copies[-1].start()
    return copies


def prefetched(weight, rows, parts=2):
    def kernel(weight_ref, out_ref, sems):
        for copy in streamed(weight_ref, out_ref, sems, 0, parts):
            copy.wait()

    return pl.pallas_call(
        kernel,
        out_shape=pltpu.VMEM((rows, weight.shape[1]), weight.dtype),
        in_specs=[hbm_block()],
        out_specs=whole_block(),
        scratch_shapes=[pltpu.SemaphoreType.DMA((parts,))],
        compiler_params=pltpu.CompilerParams(vmem_limit_bytes=VMEM_LIMIT),
        cost_estimate=NO_COST,
    )(in_hbm(weight))


def slope_rows(pieces, weight, tile=1024):
    rows = sum(piece.shape[0] for piece in pieces)
    features, width = weight.shape

    def kernel(*refs):
        *piece_refs, weight_ref, out_ref, rows_ref = refs
        assemble(piece_refs, rows_ref)
        for start in range(0, width, tile):
            cols = pl.ds(start, tile)
            preact = jnp.dot(
                rows_ref[...], weight_ref[:, cols], preferred_element_type=jnp.float32
            )
            out_ref[:, cols] = gelu_slope(preact)

    return pl.pallas_call(
        kernel,
        out_shape=jax.ShapeDtypeStruct((rows, width), jnp.float32),
        in_specs=[whole_block()] * (len(pieces) + 1),
        out_specs=whole_block(),
        scratch_shapes=[pltpu.VMEM((rows, features), jnp.bfloat16)],
        compiler_params=pltpu.CompilerParams(vmem_limit_bytes=VMEM_LIMIT),
        cost_estimate=NO_COST,
    )(*pieces, in_vmem(weight))


def scaled_rows(pieces, head, weight, slope, back, count, parts=2):
    rows, width = slope.shape
    features = weight.shape[1]
    first = head.shape[0]

    def kernel(expert_ref, *refs):
        *piece_refs, head_ref, weight_ref, slope_ref, back_ref = refs[: len(pieces) + 4]
        out_ref, kept_ref, sent_ref, rest_ref = refs[len(pieces) + 4 : len(pieces) + 8]
        rows_ref, gate_ref, held_ref, held_back_ref, sems, back_sems, rest_sems = refs[
            len(pieces) + 8 :
        ]
        copies = streamed(weight_ref, held_ref, sems, first, parts)
        assemble(piece_refs, rows_ref)
        start = 0
        for piece in piece_refs:
            gates = piece[:, features:].astype(jnp.float32)
            lane = lax.broadcasted_iota(jnp.int32, gates.shape, 1)
            gate_ref[pl.ds(start, piece.shape[0]), :] = jnp.sum(
                jnp.where(lane == expert_ref[0], gates, 0.0), axis=1, keepdims=True
            )
            start += piece.shape[0]

        def scale(block, cols):
            hidden_grad = lax.dot_general(
                rows_ref[...], block, NT, preferred_element_type=jnp.float32
            )
            out_ref[:, cols] = (gate_ref[...] * hidden_grad * slope_ref[:, cols]).astype(
                jnp.bfloat16
            )

        size = (width - first) // parts
        for start in range(0, first, size):
            scale(head_ref[pl.ds(start, size), :], pl.ds(start, size))
        back_copies = streamed(back_ref, held_back_ref, back_sems, 0, parts)
        for part, copy in enumerate(copies):
            copy.wait()
            scale(held_ref[pl.ds(part * size, size), :], pl.ds(first + part * size, size))
        rest_copies = streamed(back_ref, rest_ref, rest_sems, count, 1)
        partial_product(out_ref, held_back_ref, back_copies, (kept_ref, sent_ref))
        for copy in rest_copies:
            copy.wait()

    expert = lax.axis_index("expert").astype(jnp.int32).reshape(1)
    half = jax.ShapeDtypeStruct((rows // CORES, count), jnp.bfloat16)
    return pl.pallas_call(
        kernel,
        out_shape=[
            jax.ShapeDtypeStruct((rows, width), jnp.bfloat16),
            half,
            half,
            pltpu.VMEM((features - count, width), back.dtype),
        ],
        in_specs=[pl.BlockSpec(memory_space=pltpu.SMEM)]
        + [whole_block()] * (len(pieces) + 1)
        + [hbm_block(), whole_block(), hbm_block()],
        out_specs=[whole_block()] * 4,
        scratch_shapes=[
            pltpu.VMEM((rows, features), jnp.bfloat16),
            pltpu.VMEM((rows, 1), jnp.float32),
            pltpu.VMEM((width - first, features), weight.dtype),
            pltpu.VMEM((count, width), back.dtype),
            pltpu.SemaphoreType.DMA((parts,)),
            pltpu.SemaphoreType.DMA((parts,)),
            pltpu.SemaphoreType.DMA((1,)),
        ],
        compiler_params=pltpu.CompilerParams(vmem_limit_bytes=VMEM_LIMIT),
        cost_estimate=NO_COST,
    )(expert, *pieces, in_vmem(head), in_hbm(weight), slope, in_hbm(back))


def partial_product(scaled_ref, weight_ref, copies, out_refs):
    half = scaled_ref.shape[0] // len(out_refs)
    tile = weight_ref.shape[0] // len(copies)
    for step, copy in enumerate(copies):
        cols = pl.ds(step * tile, tile)
        if copy is not None:
            copy.wait()
        product = lax.dot_general(
            scaled_ref[...], weight_ref[cols, :], NT, preferred_element_type=jnp.float32
        ).astype(jnp.bfloat16)
        for place, out_ref in enumerate(out_refs):
            out_ref[:, cols] = product[place * half : (place + 1) * half]


def partial_rows(scaled, weight):
    rows, count = scaled.shape[0], weight.shape[0]

    def kernel(scaled_ref, weight_ref, kept_ref, sent_ref):
        partial_product(scaled_ref, weight_ref, [None], (kept_ref, sent_ref))

    half = jax.ShapeDtypeStruct((rows // CORES, count), jnp.bfloat16)
    return pl.pallas_call(
        kernel,
        out_shape=[half, half],
        in_specs=[whole_block()] * 2,
        out_specs=[whole_block()] * 2,
        compiler_params=pltpu.CompilerParams(vmem_limit_bytes=VMEM_LIMIT),
        cost_estimate=NO_COST,
    )(scaled, in_vmem(weight))


def beside(array, axis, step):
    size = lax.axis_size(axis)
    return lax.ppermute(array, axis, [(i, i ^ step) for i in range(size)])


def scatter_rows(kept, sent, rows):
    kept, sent = added([kept, beside(sent, "tensor", 1)], [rows * EXPERTS] * 2)
    kept, *sent = added([kept, beside(sent, "tensor", CORES)], [rows] * EXPERTS)
    return [kept] + [beside(block, "expert", step) for step, block in zip((*FAR, NEAR), sent)]


def dense(tokens_in, out_grad, expert_ids, gate_probs, w_in, w_out):
    local_rows, features = tokens_in.shape
    together = lax.optimization_barrier
    w_in, w_out = w_in[0], w_out[0]

    grads, both = with_gates(tokens_in, out_grad, expert_ids, gate_probs)
    *far_tokens, near, across, grads, w_in = together(
        (
            *[beside(tokens_in, "expert", step) for step in FAR],
            beside(both, "expert", NEAR),
            beside(both, "tensor", CORES),
            grads,
            w_in,
        )
    )
    far_tokens = stacked(*far_tokens)
    far_tokens, far_tokens_across, near_across, *far_grads, held_in = together(
        (
            far_tokens,
            beside(far_tokens, "tensor", CORES),
            beside(near, "tensor", CORES),
            *[beside(grads, "expert", step) for step in FAR],
            prefetched(w_in, features),
        )
    )
    token_half = stacked(
        both, far_tokens, near, across, far_tokens_across, near_across, width=features
    )
    slope = slope_rows([token_half, beside(token_half, "tensor", 1)], held_in)
    far_grads = stacked(*far_grads)
    far_grads_across, slope = together((beside(far_grads, "tensor", CORES), slope))
    grad_half = stacked(
        both,
        far_grads,
        near,
        across,
        far_grads_across,
        near_across,
        width=grads.shape[1],
        offsets=[features, 0, features, features, 0, features],
    )
    grad_half, w_out = together((grad_half, w_out))
    grad_other, head = together(
        (beside(grad_half, "tensor", 1), prefetched(w_out, w_out.shape[0] // 2))
    )
    scaled, *halves, rest = scaled_rows(
        [grad_half, grad_other], head, w_out, slope, w_in, features // 2
    )
    chunks = [halves, partial_rows(scaled, rest)]
    return added_beside([scatter_rows(*halves, local_rows) for halves in chunks])


def local(*args):
    if lax.axis_size("expert") == EXPERTS and lax.axis_size("tensor") == 2 * CORES:
        return dense(*args)
    return routed(*args)


def solution(mesh):
    return jax.shard_map(
        local,
        mesh=mesh,
        in_specs=(
            P(("parts", "expert", "tensor"), None),
            P(("parts", "expert", "tensor"), None),
            P(("parts", "expert", "tensor"), None),
            P(("parts", "expert", "tensor"), None),
            P("expert", None, "tensor"),
            P("expert", "tensor", None),
        ),
        out_specs=P(("parts", "expert", "tensor"), None),
        check_vma=False,
    )
```

```python
import math

import jax
import jax.numpy as jnp
from jax import lax
from jax.experimental import pallas as pl
from jax.experimental.pallas import tpu as pltpu
from jax.sharding import PartitionSpec as P


def gelu_slope(value):
    coeff = math.sqrt(2.0 / math.pi)
    inner = jnp.tanh(coeff * (value + 0.044715 * value * value * value))
    return 0.5 * (1.0 + inner) + 0.5 * value * (1.0 - inner * inner) * coeff * (
        1.0 + 3.0 * 0.044715 * value * value
    )


def slot_table(route_all, experts, capacity):
    flat_ids = route_all.reshape(-1)
    pair_count = flat_ids.shape[0]
    onehot = (flat_ids[:, None] == jnp.arange(experts, dtype=jnp.int32)[None, :]).astype(jnp.int32)
    before = jnp.cumsum(onehot, axis=0) - onehot
    slot_index = jnp.sum(before * onehot, axis=1)
    target = flat_ids * capacity + slot_index
    cell_index = jnp.arange(experts * capacity, dtype=jnp.int32)
    matches = target[None, :] == cell_index[:, None]
    source = jnp.sum(
        jnp.where(matches, jnp.arange(pair_count, dtype=jnp.int32)[None, :], 0), axis=1
    )
    filled = jnp.any(matches, axis=1)
    return (target, source, filled)


def routed(tokens_in, out_grad, expert_ids, gate_probs, w_in, w_out):
    experts = lax.axis_size("expert")
    shards = lax.axis_size("tensor")
    local_rows = tokens_in.shape[0]
    features = tokens_in.shape[1]
    capacity = 3 * local_rows * shards // experts
    route_all = lax.all_gather(expert_ids, "tensor", axis=0, tiled=True)
    target, source, filled = slot_table(route_all, experts, capacity)
    inputs_all, grads_all, gates_all = (
        lax.all_gather(tokens_in, "tensor", axis=0, tiled=True),
        lax.all_gather(out_grad, "tensor", axis=0, tiled=True),
        lax.all_gather(gate_probs, "tensor", axis=0, tiled=True),
    )
    token_of = source // 2
    occupied = filled[:, None]
    send_in = jnp.where(occupied, jnp.take(inputs_all, token_of, axis=0), 0)
    send_in = send_in.reshape(experts, capacity, -1)
    send_grad = jnp.where(occupied, jnp.take(grads_all, token_of, axis=0), 0)
    send_grad = send_grad.reshape(experts, capacity, -1)
    send_gate = jnp.where(filled, jnp.take(gates_all.reshape(-1), source), 0)
    send_gate = send_gate.reshape(experts, capacity)
    rows_in = lax.all_to_all(send_in, "expert", split_axis=0, concat_axis=0, tiled=True)
    rows_grad = lax.all_to_all(send_grad, "expert", split_axis=0, concat_axis=0, tiled=True)
    rows_gate = lax.all_to_all(send_gate, "expert", split_axis=0, concat_axis=0, tiled=True)
    slot_count = rows_in.shape[1]
    flat_in = rows_in.reshape(-1, features)
    flat_grad = rows_grad.reshape(-1, features)
    preact = jnp.dot(flat_in, w_in[0], preferred_element_type=jnp.float32)
    hidden_grad = jnp.einsum("rd,hd->rh", flat_grad, w_out[0], preferred_element_type=jnp.float32)
    scaled = (
        rows_gate.reshape(-1, 1).astype(jnp.float32) * hidden_grad * gelu_slope(preact)
    ).astype(jnp.bfloat16)
    partial_rows = jnp.einsum(
        "rh,dh->rd", scaled, w_in[0], preferred_element_type=jnp.float32
    ).astype(jnp.bfloat16)
    summed = lax.psum(partial_rows, "tensor").astype(jnp.float32)
    outgoing = summed.astype(jnp.bfloat16).reshape(experts, slot_count, -1)
    returned = lax.all_to_all(outgoing, "expert", split_axis=0, concat_axis=0, tiled=True)
    row_table = returned.reshape(experts * capacity, -1)
    offset_row = lax.axis_index("tensor") * (2 * local_rows)
    own_rows = lax.dynamic_slice_in_dim(target, offset_row, 2 * local_rows)
    picked = (
        jnp.take(row_table, own_rows, axis=0).astype(jnp.float32).reshape(local_rows, 2, features)
    )
    return jnp.sum(picked, axis=1).astype(jnp.bfloat16)


CORES = 2
EXPERTS = 4
NEAR, FAR = 1, (2, 3)
LANES = 128
NT = (((1,), (1,)), ((), ()))
VMEM_LIMIT = 10 * 2**20
NO_COST = pl.CostEstimate(flops=0, bytes_accessed=0, transcendentals=0)


def in_vmem(array):
    return pltpu.with_memory_space_constraint(array, pltpu.VMEM)


def whole_block():
    return pl.BlockSpec(memory_space=pltpu.VMEM)


def after(array, *earlier):
    return lax.optimization_barrier((array, *earlier))[0]


def assemble(pieces, rows_ref):
    start = 0
    for piece in pieces:
        rows_ref[pl.ds(start, piece.shape[0]), :] = piece[:, : rows_ref.shape[1]]
        start += piece.shape[0]


def small_kernel(kernel, out_shape, operands):
    return pl.pallas_call(
        kernel,
        out_shape=out_shape,
        in_specs=[whole_block()] * len(operands),
        out_specs=jax.tree.map(lambda _: whole_block(), out_shape),
        compiler_params=pltpu.CompilerParams(vmem_limit_bytes=VMEM_LIMIT),
        cost_estimate=NO_COST,
    )(*operands)


def stacked(*pieces, width=None, offsets=None):
    width = width or pieces[0].shape[1]
    offsets = offsets or [0] * len(pieces)
    rows = sum(piece.shape[0] for piece in pieces)

    def kernel(*refs):
        out_ref = refs[-1]
        start = 0
        for piece, offset in zip(refs, offsets):
            out_ref[pl.ds(start, piece.shape[0]), :] = piece[:, offset : offset + width]
            start += piece.shape[0]

    return small_kernel(kernel, jax.ShapeDtypeStruct((rows, width), jnp.bfloat16), pieces)


def added(terms, sizes):
    width = terms[0].shape[1]

    def kernel(*refs):
        term_refs, out_refs = refs[: len(terms)], refs[len(terms) :]
        start = 0
        for out_ref in out_refs:
            rows = pl.ds(start, out_ref.shape[0])
            total = term_refs[0][rows, :].astype(jnp.float32)
            for term_ref in term_refs[1:]:
                total += term_ref[rows, :].astype(jnp.float32)
            out_ref[...] = total.astype(jnp.bfloat16)
            start += out_ref.shape[0]

    return small_kernel(
        kernel, [jax.ShapeDtypeStruct((size, width), jnp.bfloat16) for size in sizes], terms
    )


def added_beside(chunks):
    rows = chunks[0][0].shape[0]
    widths = [chunk[0].shape[1] for chunk in chunks]
    terms = [term for chunk in chunks for term in chunk]

    def kernel(*refs):
        *term_refs, out_ref = refs
        start = 0
        for chunk, width in zip(chunks, widths):
            group, term_refs = term_refs[: len(chunk)], term_refs[len(chunk) :]
            total = group[0][...].astype(jnp.float32)
            for term_ref in group[1:]:
                total += term_ref[...].astype(jnp.float32)
            out_ref[:, start : start + width] = total.astype(jnp.bfloat16)
            start += width

    return small_kernel(kernel, jax.ShapeDtypeStruct((rows, sum(widths)), jnp.bfloat16), terms)


def in_hbm(array):
    return pltpu.with_memory_space_constraint(array, pltpu.HBM)


def hbm_block():
    return pl.BlockSpec(memory_space=pltpu.HBM)


def with_gates(tokens, grads, expert_ids, gate_probs):
    rows, features = grads.shape

    def kernel(tokens_ref, grads_ref, ids_ref, probs_ref, out_ref, both_ref, ids, probs, sems):
        copies = [
            pltpu.make_async_copy(source, target, sems.at[place])
            for place, (source, target) in enumerate(
                (
                    (ids_ref, ids),
                    (probs_ref, probs),
                    (tokens_ref, both_ref.at[:, pl.ds(0, features)]),
                    (grads_ref, both_ref.at[:, pl.ds(features, features)]),
                    (grads_ref, out_ref.at[:, pl.ds(0, features)]),
                )
            )
        ]
        for copy in copies:
            copy.start()
        copies[0].wait()
        copies[1].wait()
        lane = lax.broadcasted_iota(jnp.int32, (rows, LANES), 1)
        here = lax.broadcasted_iota(jnp.int32, (rows, rows), 0) == lax.broadcasted_iota(
            jnp.int32, (rows, rows), 1
        )
        upright = lambda row: jnp.sum(jnp.where(here, row, 0.0), axis=1, keepdims=True)
        gates = jnp.zeros((rows, LANES), jnp.float32)
        for k in range(ids.shape[0]):
            named = upright(ids[k : k + 1, :].astype(jnp.float32)).astype(jnp.int32)
            prob = upright(probs[k : k + 1, :].astype(jnp.float32))
            gates += jnp.where(lane == named, prob, 0.0)
        out_ref[:, features:] = gates.astype(jnp.bfloat16)
        both_ref[:, 2 * features :] = gates.astype(jnp.bfloat16)
        for copy in copies[2:]:
            copy.wait()

    return pl.pallas_call(
        kernel,
        out_shape=[
            jax.ShapeDtypeStruct((rows, features + LANES), jnp.bfloat16),
            jax.ShapeDtypeStruct((rows, 2 * features + LANES), jnp.bfloat16),
        ],
        in_specs=[hbm_block()] * 4,
        out_specs=[whole_block()] * 2,
        scratch_shapes=[
            pltpu.VMEM(expert_ids.shape[::-1], expert_ids.dtype),
            pltpu.VMEM(gate_probs.shape[::-1], gate_probs.dtype),
            pltpu.SemaphoreType.DMA((5,)),
        ],
        compiler_params=pltpu.CompilerParams(vmem_limit_bytes=VMEM_LIMIT),
        cost_estimate=NO_COST,
    )(in_hbm(tokens), in_hbm(grads), in_hbm(expert_ids.T), in_hbm(gate_probs.T))


def streamed(source_ref, target_ref, sems, first, parts, axis=0):
    size = target_ref.shape[axis] // parts
    copies = []
    for part in range(parts):
        here, there = pl.ds(first + part * size, size), pl.ds(part * size, size)
        if axis == 0:
            ends = source_ref.at[here], target_ref.at[there]
        else:
            ends = source_ref.at[:, here], target_ref.at[:, there]
        copies.append(pltpu.make_async_copy(*ends, sems.at[part]))
        copies[-1].start()
    return copies


def prefetched(weight, rows, parts=2):
    def kernel(weight_ref, out_ref, sems):
        for copy in streamed(weight_ref, out_ref, sems, 0, parts):
            copy.wait()

    return pl.pallas_call(
        kernel,
        out_shape=pltpu.VMEM((rows, weight.shape[1]), weight.dtype),
        in_specs=[hbm_block()],
        out_specs=whole_block(),
        scratch_shapes=[pltpu.SemaphoreType.DMA((parts,))],
        compiler_params=pltpu.CompilerParams(vmem_limit_bytes=VMEM_LIMIT),
        cost_estimate=NO_COST,
    )(in_hbm(weight))


def slope_rows(pieces, weight, later, head, tile=1024):
    rows = sum(piece.shape[0] for piece in pieces)
    features, width = weight.shape

    def kernel(*refs):
        *piece_refs, weight_ref, later_ref, out_ref, head_ref, rows_ref, sems = refs
        copies = streamed(later_ref, head_ref, sems, 0, 1)
        assemble(piece_refs, rows_ref)
        for start in range(0, width, tile):
            cols = pl.ds(start, tile)
            preact = jnp.dot(
                rows_ref[...], weight_ref[:, cols], preferred_element_type=jnp.float32
            )
            out_ref[:, cols] = gelu_slope(preact)
        for copy in copies:
            copy.wait()

    return pl.pallas_call(
        kernel,
        out_shape=[
            jax.ShapeDtypeStruct((rows, width), jnp.float32),
            pltpu.VMEM((head, later.shape[1]), later.dtype),
        ],
        in_specs=[whole_block()] * (len(pieces) + 1) + [hbm_block()],
        out_specs=[whole_block()] * 2,
        scratch_shapes=[
            pltpu.VMEM((rows, features), jnp.bfloat16),
            pltpu.SemaphoreType.DMA((1,)),
        ],
        compiler_params=pltpu.CompilerParams(vmem_limit_bytes=VMEM_LIMIT),
        cost_estimate=NO_COST,
    )(*pieces, in_vmem(weight), in_hbm(later))


def scaled_rows(pieces, expert, weight, slope, back, count, tile=1024):
    rows, width = slope.shape
    features = weight.shape[1]

    def kernel(expert_ref, *refs):
        *piece_refs, weight_ref, slope_ref, back_ref, out_ref, kept_ref, sent_ref = refs[:-2]
        rows_ref, gate_ref = refs[-2:]
        assemble(piece_refs, rows_ref)
        start = 0
        for piece in piece_refs:
            gates = piece[:, features:].astype(jnp.float32)
            lane = lax.broadcasted_iota(jnp.int32, gates.shape, 1)
            gate_ref[pl.ds(start, piece.shape[0]), :] = jnp.sum(
                jnp.where(lane == expert_ref[0], gates, 0.0), axis=1, keepdims=True
            )
            start += piece.shape[0]
        for start in range(0, width, tile):
            cols = pl.ds(start, tile)
            hidden_grad = lax.dot_general(
                rows_ref[...], weight_ref[cols, :], NT, preferred_element_type=jnp.float32
            )
            out_ref[:, cols] = (gate_ref[...] * hidden_grad * slope_ref[:, cols]).astype(
                jnp.bfloat16
            )
        partial_product(out_ref, back_ref, 0, (kept_ref, sent_ref))

    half = jax.ShapeDtypeStruct((rows // CORES, count), jnp.bfloat16)
    return pl.pallas_call(
        kernel,
        out_shape=[jax.ShapeDtypeStruct((rows, width), jnp.bfloat16), half, half],
        in_specs=[pl.BlockSpec(memory_space=pltpu.SMEM)] + [whole_block()] * (len(pieces) + 3),
        out_specs=[whole_block()] * 3,
        scratch_shapes=[
            pltpu.VMEM((rows, features), jnp.bfloat16),
            pltpu.VMEM((rows, 1), jnp.float32),
        ],
        compiler_params=pltpu.CompilerParams(vmem_limit_bytes=VMEM_LIMIT),
        cost_estimate=NO_COST,
    )(expert, *pieces, in_vmem(weight), slope, in_vmem(back))


def partial_product(scaled_ref, weight_ref, first, out_refs):
    half, count = out_refs[0].shape
    product = lax.dot_general(
        scaled_ref[...],
        weight_ref[pl.ds(first, count), :],
        NT,
        preferred_element_type=jnp.float32,
    ).astype(jnp.bfloat16)
    for place, out_ref in enumerate(out_refs):
        out_ref[...] = product[place * half : (place + 1) * half]


def partial_rows(scaled, weight, first):
    rows, count = scaled.shape[0], weight.shape[0] - first

    def kernel(scaled_ref, weight_ref, kept_ref, sent_ref):
        partial_product(scaled_ref, weight_ref, first, (kept_ref, sent_ref))

    half = jax.ShapeDtypeStruct((rows // CORES, count), jnp.bfloat16)
    return pl.pallas_call(
        kernel,
        out_shape=[half, half],
        in_specs=[whole_block()] * 2,
        out_specs=[whole_block()] * 2,
        compiler_params=pltpu.CompilerParams(vmem_limit_bytes=VMEM_LIMIT),
        cost_estimate=NO_COST,
    )(scaled, in_vmem(weight))


def beside(array, axis, step):
    size = lax.axis_size(axis)
    return lax.ppermute(array, axis, [(i, i ^ step) for i in range(size)])


def scatter_rows(kept, sent, rows):
    kept, sent = added([kept, beside(sent, "tensor", 1)], [rows * EXPERTS] * 2)
    kept, *sent = added([kept, beside(sent, "tensor", CORES)], [rows] * EXPERTS)
    return [kept] + [beside(block, "expert", step) for step, block in zip((*FAR, NEAR), sent)]


def dense(tokens_in, out_grad, expert_ids, gate_probs, w_in, w_out):
    local_rows, features = tokens_in.shape
    together = lax.optimization_barrier
    w_in, w_out = w_in[0], w_out[0]

    grads, both = with_gates(tokens_in, out_grad, expert_ids, gate_probs)
    expert = lax.axis_index("expert").astype(jnp.int32).reshape(1)
    *far_tokens, near, across, grads, w_in, expert = together(
        (
            *[beside(tokens_in, "expert", step) for step in FAR],
            beside(both, "expert", NEAR),
            beside(both, "tensor", CORES),
            grads,
            w_in,
            expert,
        )
    )
    far_tokens = stacked(*far_tokens)
    far_tokens, far_tokens_across, near_across, *far_grads, held_in = together(
        (
            far_tokens,
            beside(far_tokens, "tensor", CORES),
            beside(near, "tensor", CORES),
            *[beside(grads, "expert", step) for step in FAR],
            prefetched(w_in, features),
        )
    )
    token_half = stacked(
        both, far_tokens, near, across, far_tokens_across, near_across, width=features
    )
    slope, held_out = slope_rows(
        [token_half, beside(token_half, "tensor", 1)], held_in, w_out, w_out.shape[0]
    )
    far_grads = stacked(*far_grads)
    far_grads_across, slope = together((beside(far_grads, "tensor", CORES), slope))
    grad_half = stacked(
        both,
        far_grads,
        near,
        across,
        far_grads_across,
        near_across,
        width=grads.shape[1],
        offsets=[features, 0, features, features, 0, features],
    )
    grad_other = beside(grad_half, "tensor", 1)
    count = features // 2
    scaled, *halves = scaled_rows(
        [grad_half, grad_other], expert, held_out, slope, held_in, count
    )
    chunks = [halves, partial_rows(scaled, held_in, count)]
    return added_beside([scatter_rows(*halves, local_rows) for halves in chunks])


def local(*args):
    if lax.axis_size("expert") == EXPERTS and lax.axis_size("tensor") == 2 * CORES:
        return dense(*args)
    return routed(*args)


def solution(mesh):
    return jax.shard_map(
        local,
        mesh=mesh,
        in_specs=(
            P(("parts", "expert", "tensor"), None),
            P(("parts", "expert", "tensor"), None),
            P(("parts", "expert", "tensor"), None),
            P(("parts", "expert", "tensor"), None),
            P("expert", None, "tensor"),
            P("expert", "tensor", None),
        ),
        out_specs=P(("parts", "expert", "tensor"), None),
        check_vma=False,
    )
```

```python
import math

import jax
import jax.numpy as jnp
from jax import lax
from jax.experimental import pallas as pl
from jax.experimental.pallas import tpu as pltpu
from jax.sharding import PartitionSpec as P


def gelu_slope(value):
    coeff = math.sqrt(2.0 / math.pi)
    inner = jnp.tanh(coeff * (value + 0.044715 * value * value * value))
    return 0.5 * (1.0 + inner) + 0.5 * value * (1.0 - inner * inner) * coeff * (
        1.0 + 3.0 * 0.044715 * value * value
    )


def slot_table(route_all, experts, capacity):
    flat_ids = route_all.reshape(-1)
    pair_count = flat_ids.shape[0]
    onehot = (flat_ids[:, None] == jnp.arange(experts, dtype=jnp.int32)[None, :]).astype(jnp.int32)
    before = jnp.cumsum(onehot, axis=0) - onehot
    slot_index = jnp.sum(before * onehot, axis=1)
    target = flat_ids * capacity + slot_index
    cell_index = jnp.arange(experts * capacity, dtype=jnp.int32)
    matches = target[None, :] == cell_index[:, None]
    source = jnp.sum(
        jnp.where(matches, jnp.arange(pair_count, dtype=jnp.int32)[None, :], 0), axis=1
    )
    filled = jnp.any(matches, axis=1)
    return (target, source, filled)


def routed(tokens_in, out_grad, expert_ids, gate_probs, w_in, w_out):
    experts = lax.axis_size("expert")
    shards = lax.axis_size("tensor")
    local_rows = tokens_in.shape[0]
    features = tokens_in.shape[1]
    capacity = 3 * local_rows * shards // experts
    route_all = lax.all_gather(expert_ids, "tensor", axis=0, tiled=True)
    target, source, filled = slot_table(route_all, experts, capacity)
    inputs_all, grads_all, gates_all = (
        lax.all_gather(tokens_in, "tensor", axis=0, tiled=True),
        lax.all_gather(out_grad, "tensor", axis=0, tiled=True),
        lax.all_gather(gate_probs, "tensor", axis=0, tiled=True),
    )
    token_of = source // 2
    occupied = filled[:, None]
    send_in = jnp.where(occupied, jnp.take(inputs_all, token_of, axis=0), 0)
    send_in = send_in.reshape(experts, capacity, -1)
    send_grad = jnp.where(occupied, jnp.take(grads_all, token_of, axis=0), 0)
    send_grad = send_grad.reshape(experts, capacity, -1)
    send_gate = jnp.where(filled, jnp.take(gates_all.reshape(-1), source), 0)
    send_gate = send_gate.reshape(experts, capacity)
    rows_in = lax.all_to_all(send_in, "expert", split_axis=0, concat_axis=0, tiled=True)
    rows_grad = lax.all_to_all(send_grad, "expert", split_axis=0, concat_axis=0, tiled=True)
    rows_gate = lax.all_to_all(send_gate, "expert", split_axis=0, concat_axis=0, tiled=True)
    slot_count = rows_in.shape[1]
    flat_in = rows_in.reshape(-1, features)
    flat_grad = rows_grad.reshape(-1, features)
    preact = jnp.dot(flat_in, w_in[0], preferred_element_type=jnp.float32)
    hidden_grad = jnp.einsum("rd,hd->rh", flat_grad, w_out[0], preferred_element_type=jnp.float32)
    scaled = (
        rows_gate.reshape(-1, 1).astype(jnp.float32) * hidden_grad * gelu_slope(preact)
    ).astype(jnp.bfloat16)
    partial_rows = jnp.einsum(
        "rh,dh->rd", scaled, w_in[0], preferred_element_type=jnp.float32
    ).astype(jnp.bfloat16)
    summed = lax.psum(partial_rows, "tensor").astype(jnp.float32)
    outgoing = summed.astype(jnp.bfloat16).reshape(experts, slot_count, -1)
    returned = lax.all_to_all(outgoing, "expert", split_axis=0, concat_axis=0, tiled=True)
    row_table = returned.reshape(experts * capacity, -1)
    offset_row = lax.axis_index("tensor") * (2 * local_rows)
    own_rows = lax.dynamic_slice_in_dim(target, offset_row, 2 * local_rows)
    picked = (
        jnp.take(row_table, own_rows, axis=0).astype(jnp.float32).reshape(local_rows, 2, features)
    )
    return jnp.sum(picked, axis=1).astype(jnp.bfloat16)


CORES = 2
EXPERTS = 4
NEAR, FAR = 1, (2, 3)
LANES = 128
NT = (((1,), (1,)), ((), ()))
VMEM_LIMIT = 10 * 2**20
NO_COST = pl.CostEstimate(flops=0, bytes_accessed=0, transcendentals=0)
LONG = pl.CostEstimate(flops=10**11, bytes_accessed=10**9, transcendentals=0)


def in_vmem(array):
    return pltpu.with_memory_space_constraint(array, pltpu.VMEM)


def whole_block():
    return pl.BlockSpec(memory_space=pltpu.VMEM)


def after(array, *earlier):
    return lax.optimization_barrier((array, *earlier))[0]


def assemble(pieces, rows_ref):
    start = 0
    for piece in pieces:
        rows_ref[pl.ds(start, piece.shape[0]), :] = piece[:, : rows_ref.shape[1]]
        start += piece.shape[0]


def small_kernel(kernel, out_shape, operands, cost=NO_COST):
    return pl.pallas_call(
        kernel,
        out_shape=out_shape,
        in_specs=[whole_block()] * len(operands),
        out_specs=jax.tree.map(lambda _: whole_block(), out_shape),
        compiler_params=pltpu.CompilerParams(vmem_limit_bytes=VMEM_LIMIT),
        cost_estimate=cost,
    )(*operands)


def stacked(*pieces, width=None, offsets=None, cost=NO_COST):
    width = width or pieces[0].shape[1]
    offsets = offsets or [0] * len(pieces)
    rows = sum(piece.shape[0] for piece in pieces)

    def kernel(*refs):
        out_ref = refs[-1]
        start = 0
        for piece, offset in zip(refs, offsets):
            out_ref[pl.ds(start, piece.shape[0]), :] = piece[:, offset : offset + width]
            start += piece.shape[0]

    return small_kernel(kernel, jax.ShapeDtypeStruct((rows, width), jnp.bfloat16), pieces, cost)


def passed(*arrays, cost=NO_COST):
    def kernel(*refs):
        for array_ref, out_ref in zip(refs[: len(arrays)], refs[len(arrays) :]):
            out_ref[...] = array_ref[...]

    out_shape = [jax.ShapeDtypeStruct(array.shape, array.dtype) for array in arrays]
    return small_kernel(kernel, out_shape, arrays, cost)


def added(terms, sizes, joined=None, cost=NO_COST):
    width = terms[0].shape[1]
    widths = [width] * len(sizes)
    if joined is not None:
        widths[-1] += joined.shape[1]

    def kernel(*refs):
        term_refs, out_refs = refs[: len(terms)], refs[-len(sizes) :]
        start = 0
        for out_ref in out_refs:
            rows = pl.ds(start, out_ref.shape[0])
            total = term_refs[0][rows, :].astype(jnp.float32)
            for term_ref in term_refs[1:]:
                total += term_ref[rows, :].astype(jnp.float32)
            out_ref[:, out_ref.shape[1] - width :] = total.astype(jnp.bfloat16)
            start += out_ref.shape[0]
        if joined is not None:
            out_refs[-1][:, : joined.shape[1]] = refs[len(terms)][...]

    return small_kernel(
        kernel,
        [jax.ShapeDtypeStruct((size, wide), jnp.bfloat16) for size, wide in zip(sizes, widths)],
        terms if joined is None else [*terms, joined],
        cost,
    )


def added_beside(chunks, wide):
    rows = chunks[0][0].shape[0]
    widths = [chunk[0].shape[1] for chunk in chunks]
    terms = [term for chunk in chunks for term in chunk]

    def kernel(*refs):
        *term_refs, wide_ref, out_ref = refs
        start = 0
        for chunk, width in zip(chunks, widths):
            group, term_refs = term_refs[: len(chunk)], term_refs[len(chunk) :]
            total = wide_ref[:, start : start + width].astype(jnp.float32)
            for term_ref in group:
                total += term_ref[...].astype(jnp.float32)
            out_ref[:, start : start + width] = total.astype(jnp.bfloat16)
            start += width

    return small_kernel(
        kernel, jax.ShapeDtypeStruct((rows, sum(widths)), jnp.bfloat16), [*terms, wide]
    )


def in_hbm(array):
    return pltpu.with_memory_space_constraint(array, pltpu.HBM)


def hbm_block():
    return pl.BlockSpec(memory_space=pltpu.HBM)


def with_gates(tokens, grads, expert_ids, gate_probs):
    rows, features = grads.shape

    def kernel(tokens_ref, grads_ref, ids_ref, probs_ref, out_ref, both_ref, ids, probs, sems):
        copies = [
            pltpu.make_async_copy(source, target, sems.at[place])
            for place, (source, target) in enumerate(
                (
                    (ids_ref, ids),
                    (probs_ref, probs),
                    (tokens_ref, both_ref.at[:, pl.ds(0, features)]),
                    (grads_ref, both_ref.at[:, pl.ds(features, features)]),
                    (grads_ref, out_ref.at[:, pl.ds(0, features)]),
                )
            )
        ]
        for copy in copies:
            copy.start()
        copies[0].wait()
        copies[1].wait()
        lane = lax.broadcasted_iota(jnp.int32, (rows, LANES), 1)
        here = lax.broadcasted_iota(jnp.int32, (rows, rows), 0) == lax.broadcasted_iota(
            jnp.int32, (rows, rows), 1
        )
        upright = lambda row: jnp.sum(jnp.where(here, row, 0.0), axis=1, keepdims=True)
        gates = jnp.zeros((rows, LANES), jnp.float32)
        for k in range(ids.shape[0]):
            named = upright(ids[k : k + 1, :].astype(jnp.float32)).astype(jnp.int32)
            prob = upright(probs[k : k + 1, :].astype(jnp.float32))
            gates += jnp.where(lane == named, prob, 0.0)
        out_ref[:, features:] = gates.astype(jnp.bfloat16)
        both_ref[:, 2 * features :] = gates.astype(jnp.bfloat16)
        for copy in copies[2:]:
            copy.wait()

    return pl.pallas_call(
        kernel,
        out_shape=[
            jax.ShapeDtypeStruct((rows, features + LANES), jnp.bfloat16),
            jax.ShapeDtypeStruct((rows, 2 * features + LANES), jnp.bfloat16),
        ],
        in_specs=[hbm_block()] * 4,
        out_specs=[whole_block()] * 2,
        scratch_shapes=[
            pltpu.VMEM(expert_ids.shape[::-1], expert_ids.dtype),
            pltpu.VMEM(gate_probs.shape[::-1], gate_probs.dtype),
            pltpu.SemaphoreType.DMA((5,)),
        ],
        compiler_params=pltpu.CompilerParams(vmem_limit_bytes=VMEM_LIMIT),
        cost_estimate=NO_COST,
    )(in_hbm(tokens), in_hbm(grads), in_hbm(expert_ids.T), in_hbm(gate_probs.T))


def streamed(source_ref, target_ref, sems, first, parts, axis=0):
    size = target_ref.shape[axis] // parts
    copies = []
    for part in range(parts):
        here, there = pl.ds(first + part * size, size), pl.ds(part * size, size)
        if axis == 0:
            ends = source_ref.at[here], target_ref.at[there]
        else:
            ends = source_ref.at[:, here], target_ref.at[:, there]
        copies.append(pltpu.make_async_copy(*ends, sems.at[part]))
        copies[-1].start()
    return copies


def prefetched(weight, rows, parts=2):
    def kernel(weight_ref, out_ref, sems):
        for copy in streamed(weight_ref, out_ref, sems, 0, parts):
            copy.wait()

    return pl.pallas_call(
        kernel,
        out_shape=pltpu.VMEM((rows, weight.shape[1]), weight.dtype),
        in_specs=[hbm_block()],
        out_specs=whole_block(),
        scratch_shapes=[pltpu.SemaphoreType.DMA((parts,))],
        compiler_params=pltpu.CompilerParams(vmem_limit_bytes=VMEM_LIMIT),
        cost_estimate=NO_COST,
    )(in_hbm(weight))


def slope_rows(pieces, weight, later, head, tile=1024):
    rows = sum(piece.shape[0] for piece in pieces)
    features, width = weight.shape

    def kernel(*refs):
        *piece_refs, weight_ref, later_ref, out_ref, head_ref, rows_ref, sems = refs
        copies = streamed(later_ref, head_ref, sems, 0, 1)
        assemble(piece_refs, rows_ref)
        for start in range(0, width, tile):
            cols = pl.ds(start, tile)
            preact = jnp.dot(
                rows_ref[...], weight_ref[:, cols], preferred_element_type=jnp.float32
            )
            out_ref[:, cols] = gelu_slope(preact)
        for copy in copies:
            copy.wait()

    return pl.pallas_call(
        kernel,
        out_shape=[
            jax.ShapeDtypeStruct((rows, width), jnp.float32),
            pltpu.VMEM((head, later.shape[1]), later.dtype),
        ],
        in_specs=[whole_block()] * (len(pieces) + 1) + [hbm_block()],
        out_specs=[whole_block()] * 2,
        scratch_shapes=[
            pltpu.VMEM((rows, features), jnp.bfloat16),
            pltpu.SemaphoreType.DMA((1,)),
        ],
        compiler_params=pltpu.CompilerParams(vmem_limit_bytes=VMEM_LIMIT),
        cost_estimate=NO_COST,
    )(*pieces, in_vmem(weight), in_hbm(later))


def scaled_rows(pieces, expert, weight, slope, back, count, tile=1024):
    rows, width = slope.shape
    features = weight.shape[1]

    def kernel(expert_ref, *refs):
        *piece_refs, weight_ref, slope_ref, back_ref, out_ref, kept_ref, sent_ref = refs[:-2]
        rows_ref, gate_ref = refs[-2:]
        assemble(piece_refs, rows_ref)
        start = 0
        for piece in piece_refs:
            gates = piece[:, features:].astype(jnp.float32)
            lane = lax.broadcasted_iota(jnp.int32, gates.shape, 1)
            gate_ref[pl.ds(start, piece.shape[0]), :] = jnp.sum(
                jnp.where(lane == expert_ref[0], gates, 0.0), axis=1, keepdims=True
            )
            start += piece.shape[0]
        for start in range(0, width, tile):
            cols = pl.ds(start, tile)
            hidden_grad = lax.dot_general(
                rows_ref[...], weight_ref[cols, :], NT, preferred_element_type=jnp.float32
            )
            out_ref[:, cols] = (gate_ref[...] * hidden_grad * slope_ref[:, cols]).astype(
                jnp.bfloat16
            )
        partial_product(out_ref, back_ref, 0, (kept_ref, sent_ref))

    half = jax.ShapeDtypeStruct((rows // CORES, count), jnp.bfloat16)
    return pl.pallas_call(
        kernel,
        out_shape=[jax.ShapeDtypeStruct((rows, width), jnp.bfloat16), half, half],
        in_specs=[pl.BlockSpec(memory_space=pltpu.SMEM)] + [whole_block()] * (len(pieces) + 3),
        out_specs=[whole_block()] * 3,
        scratch_shapes=[
            pltpu.VMEM((rows, features), jnp.bfloat16),
            pltpu.VMEM((rows, 1), jnp.float32),
        ],
        compiler_params=pltpu.CompilerParams(vmem_limit_bytes=VMEM_LIMIT),
        cost_estimate=NO_COST,
    )(expert, *pieces, in_vmem(weight), slope, in_vmem(back))


def partial_product(scaled_ref, weight_ref, first, out_refs):
    half, count = out_refs[0].shape
    product = lax.dot_general(
        scaled_ref[...],
        weight_ref[pl.ds(first, count), :],
        NT,
        preferred_element_type=jnp.float32,
    ).astype(jnp.bfloat16)
    for place, out_ref in enumerate(out_refs):
        out_ref[...] = product[place * half : (place + 1) * half]


def partial_rows(scaled, weight, first):
    rows, count = scaled.shape[0], weight.shape[0] - first

    def kernel(scaled_ref, weight_ref, kept_ref, sent_ref):
        partial_product(scaled_ref, weight_ref, first, (kept_ref, sent_ref))

    half = jax.ShapeDtypeStruct((rows // CORES, count), jnp.bfloat16)
    return pl.pallas_call(
        kernel,
        out_shape=[half, half],
        in_specs=[whole_block()] * 2,
        out_specs=[whole_block()] * 2,
        compiler_params=pltpu.CompilerParams(vmem_limit_bytes=VMEM_LIMIT),
        cost_estimate=NO_COST,
    )(scaled, in_vmem(weight))


def beside(array, axis, step):
    size = lax.axis_size(axis)
    return lax.ppermute(array, axis, [(i, i ^ step) for i in range(size)])


def scatter_rows(chunks, rows):
    terms, near = [], None
    for kept, sent in chunks:
        kept, sent = added([kept, beside(sent, "tensor", 1)], [rows * EXPERTS] * 2)
        kept, *sent, near = added(
            [kept, beside(sent, "tensor", CORES)], [rows] * EXPERTS, near
        )
        terms.append([kept] + [beside(block, "expert", step) for step, block in zip(FAR, sent)])
    terms[0] = added(terms[0], [rows], cost=LONG)
    return added_beside(terms, beside(near, "expert", NEAR))


def dense(tokens_in, out_grad, expert_ids, gate_probs, w_in, w_out):
    local_rows, features = tokens_in.shape
    together = lax.optimization_barrier
    w_in, w_out = w_in[0], w_out[0]

    grads, both = with_gates(tokens_in, out_grad, expert_ids, gate_probs)
    expert = lax.axis_index("expert").astype(jnp.int32).reshape(1)
    near = beside(both, "expert", NEAR)
    across = beside(both, "tensor", CORES)
    far_tokens = passed(*[beside(tokens_in, "expert", step) for step in FAR], cost=LONG)
    *far_tokens, across, grads, w_in, expert = together((*far_tokens, across, grads, w_in, expert))
    far_grads = stacked(*[beside(grads, "expert", step) for step in FAR])
    *far_tokens_across, near_across, far_grads, held_in = together(
        (
            *[beside(tokens, "tensor", CORES) for tokens in far_tokens],
            beside(near, "tensor", CORES),
            far_grads,
            prefetched(w_in, features),
        )
    )
    token_half = stacked(
        both, *far_tokens, near, across, *far_tokens_across, near_across, width=features
    )
    slope, held_out = slope_rows(
        [token_half, beside(token_half, "tensor", 1)], held_in, w_out, w_out.shape[0]
    )
    grad_column = stacked(both, far_grads, near, width=grads.shape[1], offsets=[features, 0, features])
    far_grads_across, slope, grad_column_other = together(
        (beside(far_grads, "tensor", CORES), slope, beside(grad_column, "tensor", 1))
    )
    grad_across = stacked(
        across, far_grads_across, near_across, width=grads.shape[1], offsets=[features, 0, features]
    )
    grad_pieces = [grad_column, grad_across, grad_column_other, beside(grad_across, "tensor", 1)]
    count = features // 2
    scaled, *halves = scaled_rows(
        grad_pieces, expert, held_out, slope, held_in, count
    )
    return scatter_rows([halves, partial_rows(scaled, held_in, count)], local_rows)


def local(*args):
    if lax.axis_size("expert") == EXPERTS and lax.axis_size("tensor") == 2 * CORES:
        return dense(*args)
    return routed(*args)


def solution(mesh):
    return jax.shard_map(
        local,
        mesh=mesh,
        in_specs=(
            P(("parts", "expert", "tensor"), None),
            P(("parts", "expert", "tensor"), None),
            P(("parts", "expert", "tensor"), None),
            P(("parts", "expert", "tensor"), None),
            P("expert", None, "tensor"),
            P("expert", "tensor", None),
        ),
        out_specs=P(("parts", "expert", "tensor"), None),
        check_vma=False,
    )
```

```python
import math

import jax
import jax.numpy as jnp
from jax import lax
from jax.experimental import pallas as pl
from jax.experimental.pallas import tpu as pltpu
from jax.sharding import PartitionSpec as P


def gelu_slope(value):
    coeff = math.sqrt(2.0 / math.pi)
    inner = jnp.tanh(coeff * (value + 0.044715 * value * value * value))
    return 0.5 * (1.0 + inner) + 0.5 * value * (1.0 - inner * inner) * coeff * (
        1.0 + 3.0 * 0.044715 * value * value
    )


def slot_table(route_all, experts, capacity):
    flat_ids = route_all.reshape(-1)
    pair_count = flat_ids.shape[0]
    onehot = (flat_ids[:, None] == jnp.arange(experts, dtype=jnp.int32)[None, :]).astype(jnp.int32)
    before = jnp.cumsum(onehot, axis=0) - onehot
    slot_index = jnp.sum(before * onehot, axis=1)
    target = flat_ids * capacity + slot_index
    cell_index = jnp.arange(experts * capacity, dtype=jnp.int32)
    matches = target[None, :] == cell_index[:, None]
    source = jnp.sum(
        jnp.where(matches, jnp.arange(pair_count, dtype=jnp.int32)[None, :], 0), axis=1
    )
    filled = jnp.any(matches, axis=1)
    return (target, source, filled)


def routed(tokens_in, out_grad, expert_ids, gate_probs, w_in, w_out):
    experts = lax.axis_size("expert")
    shards = lax.axis_size("tensor")
    local_rows = tokens_in.shape[0]
    features = tokens_in.shape[1]
    capacity = 3 * local_rows * shards // experts
    route_all = lax.all_gather(expert_ids, "tensor", axis=0, tiled=True)
    target, source, filled = slot_table(route_all, experts, capacity)
    inputs_all, grads_all, gates_all = (
        lax.all_gather(tokens_in, "tensor", axis=0, tiled=True),
        lax.all_gather(out_grad, "tensor", axis=0, tiled=True),
        lax.all_gather(gate_probs, "tensor", axis=0, tiled=True),
    )
    token_of = source // 2
    occupied = filled[:, None]
    send_in = jnp.where(occupied, jnp.take(inputs_all, token_of, axis=0), 0)
    send_in = send_in.reshape(experts, capacity, -1)
    send_grad = jnp.where(occupied, jnp.take(grads_all, token_of, axis=0), 0)
    send_grad = send_grad.reshape(experts, capacity, -1)
    send_gate = jnp.where(filled, jnp.take(gates_all.reshape(-1), source), 0)
    send_gate = send_gate.reshape(experts, capacity)
    rows_in = lax.all_to_all(send_in, "expert", split_axis=0, concat_axis=0, tiled=True)
    rows_grad = lax.all_to_all(send_grad, "expert", split_axis=0, concat_axis=0, tiled=True)
    rows_gate = lax.all_to_all(send_gate, "expert", split_axis=0, concat_axis=0, tiled=True)
    slot_count = rows_in.shape[1]
    flat_in = rows_in.reshape(-1, features)
    flat_grad = rows_grad.reshape(-1, features)
    preact = jnp.dot(flat_in, w_in[0], preferred_element_type=jnp.float32)
    hidden_grad = jnp.einsum("rd,hd->rh", flat_grad, w_out[0], preferred_element_type=jnp.float32)
    scaled = (
        rows_gate.reshape(-1, 1).astype(jnp.float32) * hidden_grad * gelu_slope(preact)
    ).astype(jnp.bfloat16)
    partial_rows = jnp.einsum(
        "rh,dh->rd", scaled, w_in[0], preferred_element_type=jnp.float32
    ).astype(jnp.bfloat16)
    summed = lax.psum(partial_rows, "tensor").astype(jnp.float32)
    outgoing = summed.astype(jnp.bfloat16).reshape(experts, slot_count, -1)
    returned = lax.all_to_all(outgoing, "expert", split_axis=0, concat_axis=0, tiled=True)
    row_table = returned.reshape(experts * capacity, -1)
    offset_row = lax.axis_index("tensor") * (2 * local_rows)
    own_rows = lax.dynamic_slice_in_dim(target, offset_row, 2 * local_rows)
    picked = (
        jnp.take(row_table, own_rows, axis=0).astype(jnp.float32).reshape(local_rows, 2, features)
    )
    return jnp.sum(picked, axis=1).astype(jnp.bfloat16)


CORES = 2
EXPERTS = 4
NEAR, FAR = 1, (2, 3)
LANES = 128
NT = (((1,), (1,)), ((), ()))
VMEM_LIMIT = 10 * 2**20
NO_COST = pl.CostEstimate(flops=0, bytes_accessed=0, transcendentals=0)
LONG = pl.CostEstimate(flops=10**11, bytes_accessed=10**9, transcendentals=0)


def in_vmem(array):
    return pltpu.with_memory_space_constraint(array, pltpu.VMEM)


def whole_block():
    return pl.BlockSpec(memory_space=pltpu.VMEM)


def after(array, *earlier):
    return lax.optimization_barrier((array, *earlier))[0]


def assemble(pieces, rows_ref):
    start = 0
    for piece in pieces:
        rows_ref[pl.ds(start, piece.shape[0]), :] = piece[:, : rows_ref.shape[1]]
        start += piece.shape[0]


def small_kernel(kernel, out_shape, operands, cost=NO_COST):
    return pl.pallas_call(
        kernel,
        out_shape=out_shape,
        in_specs=[whole_block()] * len(operands),
        out_specs=jax.tree.map(lambda _: whole_block(), out_shape),
        compiler_params=pltpu.CompilerParams(vmem_limit_bytes=VMEM_LIMIT),
        cost_estimate=cost,
    )(*operands)


def stacked(*pieces, width=None, offsets=None, cost=NO_COST):
    width = width or pieces[0].shape[1]
    offsets = offsets or [0] * len(pieces)
    rows = sum(piece.shape[0] for piece in pieces)

    def kernel(*refs):
        out_ref = refs[-1]
        start = 0
        for piece, offset in zip(refs, offsets):
            out_ref[pl.ds(start, piece.shape[0]), :] = piece[:, offset : offset + width]
            start += piece.shape[0]

    return small_kernel(kernel, jax.ShapeDtypeStruct((rows, width), jnp.bfloat16), pieces, cost)


def passed(*arrays, cost=NO_COST):
    def kernel(*refs):
        for array_ref, out_ref in zip(refs[: len(arrays)], refs[len(arrays) :]):
            out_ref[...] = array_ref[...]

    out_shape = [jax.ShapeDtypeStruct(array.shape, array.dtype) for array in arrays]
    return small_kernel(kernel, out_shape, arrays, cost)


def parted(array, width, cost=NO_COST):
    def kernel(array_ref, left_ref, right_ref):
        left_ref[...] = array_ref[:, :width]
        right_ref[...] = array_ref[:, width:]

    rows, columns = array.shape
    out_shape = [
        jax.ShapeDtypeStruct((rows, width), jnp.bfloat16),
        jax.ShapeDtypeStruct((rows, columns - width), jnp.bfloat16),
    ]
    return small_kernel(kernel, out_shape, [array], cost)


def added(terms, sizes, sides=1):
    width = terms[0].shape[1]
    half = sum(sizes)

    def kernel(*refs):
        term_refs, out_refs = refs[: len(terms)], refs[len(terms) :]
        start = 0
        for size, out_ref in zip(sizes, out_refs):
            for side in range(sides):
                rows = pl.ds(side * half + start, size)
                total = term_refs[0][rows, :].astype(jnp.float32)
                for term_ref in term_refs[1:]:
                    total += term_ref[rows, :].astype(jnp.float32)
                out_ref[pl.ds(side * size, size), :] = total.astype(jnp.bfloat16)
            start += size

    out_shape = [jax.ShapeDtypeStruct((sides * size, width), jnp.bfloat16) for size in sizes]
    return small_kernel(kernel, out_shape, terms)


def added_beside(chunks):
    rows = chunks[0][0].shape[0]
    widths = [chunk[0].shape[1] for chunk in chunks]
    terms = [term for chunk in chunks for term in chunk]

    def kernel(*refs):
        *term_refs, out_ref = refs
        start = 0
        for chunk, width in zip(chunks, widths):
            group, term_refs = term_refs[: len(chunk)], term_refs[len(chunk) :]
            total = group[0][...].astype(jnp.float32)
            for term_ref in group[1:]:
                total += term_ref[...].astype(jnp.float32)
            out_ref[:, start : start + width] = total.astype(jnp.bfloat16)
            start += width

    return small_kernel(kernel, jax.ShapeDtypeStruct((rows, sum(widths)), jnp.bfloat16), terms)


def in_hbm(array):
    return pltpu.with_memory_space_constraint(array, pltpu.HBM)


def hbm_block():
    return pl.BlockSpec(memory_space=pltpu.HBM)


def with_gates(tokens, grads, expert_ids, gate_probs):
    rows, features = grads.shape

    def kernel(tokens_ref, grads_ref, ids_ref, probs_ref, out_ref, both_ref, ids, probs, sems):
        copies = [
            pltpu.make_async_copy(source, target, sems.at[place])
            for place, (source, target) in enumerate(
                (
                    (ids_ref, ids),
                    (probs_ref, probs),
                    (tokens_ref, both_ref.at[:, pl.ds(0, features)]),
                    (grads_ref, both_ref.at[:, pl.ds(features, features)]),
                    (grads_ref, out_ref.at[:, pl.ds(0, features)]),
                )
            )
        ]
        for copy in copies:
            copy.start()
        copies[0].wait()
        copies[1].wait()
        lane = lax.broadcasted_iota(jnp.int32, (rows, LANES), 1)
        here = lax.broadcasted_iota(jnp.int32, (rows, rows), 0) == lax.broadcasted_iota(
            jnp.int32, (rows, rows), 1
        )
        upright = lambda row: jnp.sum(jnp.where(here, row, 0.0), axis=1, keepdims=True)
        gates = jnp.zeros((rows, LANES), jnp.float32)
        for k in range(ids.shape[0]):
            named = upright(ids[k : k + 1, :].astype(jnp.float32)).astype(jnp.int32)
            prob = upright(probs[k : k + 1, :].astype(jnp.float32))
            gates += jnp.where(lane == named, prob, 0.0)
        out_ref[:, features:] = gates.astype(jnp.bfloat16)
        both_ref[:, 2 * features :] = gates.astype(jnp.bfloat16)
        for copy in copies[2:]:
            copy.wait()

    return pl.pallas_call(
        kernel,
        out_shape=[
            jax.ShapeDtypeStruct((rows, features + LANES), jnp.bfloat16),
            jax.ShapeDtypeStruct((rows, 2 * features + LANES), jnp.bfloat16),
        ],
        in_specs=[hbm_block()] * 4,
        out_specs=[whole_block()] * 2,
        scratch_shapes=[
            pltpu.VMEM(expert_ids.shape[::-1], expert_ids.dtype),
            pltpu.VMEM(gate_probs.shape[::-1], gate_probs.dtype),
            pltpu.SemaphoreType.DMA((5,)),
        ],
        compiler_params=pltpu.CompilerParams(vmem_limit_bytes=VMEM_LIMIT),
        cost_estimate=NO_COST,
    )(in_hbm(tokens), in_hbm(grads), in_hbm(expert_ids.T), in_hbm(gate_probs.T))


def streamed(source_ref, target_ref, sems, first, parts, axis=0):
    size = target_ref.shape[axis] // parts
    copies = []
    for part in range(parts):
        here, there = pl.ds(first + part * size, size), pl.ds(part * size, size)
        if axis == 0:
            ends = source_ref.at[here], target_ref.at[there]
        else:
            ends = source_ref.at[:, here], target_ref.at[:, there]
        copies.append(pltpu.make_async_copy(*ends, sems.at[part]))
        copies[-1].start()
    return copies


def prefetched(weight, rows, parts=2):
    def kernel(weight_ref, out_ref, sems):
        for copy in streamed(weight_ref, out_ref, sems, 0, parts):
            copy.wait()

    return pl.pallas_call(
        kernel,
        out_shape=pltpu.VMEM((rows, weight.shape[1]), weight.dtype),
        in_specs=[hbm_block()],
        out_specs=whole_block(),
        scratch_shapes=[pltpu.SemaphoreType.DMA((parts,))],
        compiler_params=pltpu.CompilerParams(vmem_limit_bytes=VMEM_LIMIT),
        cost_estimate=NO_COST,
    )(in_hbm(weight))


def slope_rows(pieces, weight, later, head, tile=1024):
    rows = sum(piece.shape[0] for piece in pieces)
    features, width = weight.shape

    def kernel(*refs):
        *piece_refs, weight_ref, later_ref, out_ref, head_ref, rows_ref, sems = refs
        copies = streamed(later_ref, head_ref, sems, 0, 1)
        assemble(piece_refs, rows_ref)
        for start in range(0, width, tile):
            cols = pl.ds(start, tile)
            preact = jnp.dot(
                rows_ref[...], weight_ref[:, cols], preferred_element_type=jnp.float32
            )
            out_ref[:, cols] = gelu_slope(preact)
        for copy in copies:
            copy.wait()

    return pl.pallas_call(
        kernel,
        out_shape=[
            jax.ShapeDtypeStruct((rows, width), jnp.float32),
            pltpu.VMEM((head, later.shape[1]), later.dtype),
        ],
        in_specs=[whole_block()] * (len(pieces) + 1) + [hbm_block()],
        out_specs=[whole_block()] * 2,
        scratch_shapes=[
            pltpu.VMEM((rows, features), jnp.bfloat16),
            pltpu.SemaphoreType.DMA((1,)),
        ],
        compiler_params=pltpu.CompilerParams(vmem_limit_bytes=VMEM_LIMIT),
        cost_estimate=NO_COST,
    )(*pieces, in_vmem(weight), in_hbm(later))


def scaled_rows(pieces, expert, weight, slope, back, count, tile=1024):
    rows, width = slope.shape
    features = weight.shape[1]

    def kernel(expert_ref, *refs):
        *piece_refs, weight_ref, slope_ref, back_ref, out_ref, kept_ref, sent_ref = refs[:-2]
        rows_ref, gate_ref = refs[-2:]
        assemble(piece_refs, rows_ref)
        start = 0
        for piece in piece_refs:
            gates = piece[:, features:].astype(jnp.float32)
            lane = lax.broadcasted_iota(jnp.int32, gates.shape, 1)
            gate_ref[pl.ds(start, piece.shape[0]), :] = jnp.sum(
                jnp.where(lane == expert_ref[0], gates, 0.0), axis=1, keepdims=True
            )
            start += piece.shape[0]
        for start in range(0, width, tile):
            cols = pl.ds(start, tile)
            hidden_grad = lax.dot_general(
                rows_ref[...], weight_ref[cols, :], NT, preferred_element_type=jnp.float32
            )
            out_ref[:, cols] = (gate_ref[...] * hidden_grad * slope_ref[:, cols]).astype(
                jnp.bfloat16
            )
        partial_product(out_ref, back_ref, 0, (kept_ref, sent_ref))

    half = jax.ShapeDtypeStruct((rows // CORES, count), jnp.bfloat16)
    return pl.pallas_call(
        kernel,
        out_shape=[jax.ShapeDtypeStruct((rows, width), jnp.bfloat16), half, half],
        in_specs=[pl.BlockSpec(memory_space=pltpu.SMEM)] + [whole_block()] * (len(pieces) + 3),
        out_specs=[whole_block()] * 3,
        scratch_shapes=[
            pltpu.VMEM((rows, features), jnp.bfloat16),
            pltpu.VMEM((rows, 1), jnp.float32),
        ],
        compiler_params=pltpu.CompilerParams(vmem_limit_bytes=VMEM_LIMIT),
        cost_estimate=NO_COST,
    )(expert, *pieces, in_vmem(weight), slope, in_vmem(back))


def partial_product(scaled_ref, weight_ref, first, out_refs):
    half, count = out_refs[0].shape
    product = lax.dot_general(
        scaled_ref[...],
        weight_ref[pl.ds(first, count), :],
        NT,
        preferred_element_type=jnp.float32,
    ).astype(jnp.bfloat16)
    for place, out_ref in enumerate(out_refs):
        out_ref[...] = product[place * half : (place + 1) * half]


def partial_rows(scaled, weight, first):
    rows, count = scaled.shape[0], weight.shape[0] - first

    def kernel(scaled_ref, weight_ref, kept_ref, sent_ref):
        partial_product(scaled_ref, weight_ref, first, (kept_ref, sent_ref))

    half = jax.ShapeDtypeStruct((rows // CORES, count), jnp.bfloat16)
    return pl.pallas_call(
        kernel,
        out_shape=[half, half],
        in_specs=[whole_block()] * 2,
        out_specs=[whole_block()] * 2,
        compiler_params=pltpu.CompilerParams(vmem_limit_bytes=VMEM_LIMIT),
        cost_estimate=NO_COST,
    )(scaled, in_vmem(weight))


def beside(array, axis, step):
    size = lax.axis_size(axis)
    return lax.ppermute(array, axis, [(i, i ^ step) for i in range(size)])


def scatter_rows(wide, narrow, rows):
    steps = (*FAR, NEAR)
    kept, sent = wide
    kept, sent = added([kept, beside(sent, "tensor", 1)], [rows * EXPERTS] * 2)
    across = beside(sent, "tensor", CORES)
    narrow_kept, narrow_sent = narrow
    blocks = added([narrow_kept, beside(narrow_sent, "tensor", 1)], [rows] * EXPERTS, sides=2)
    blocks = [blocks[0]] + [beside(block, "expert", step) for step, block in zip(steps, blocks[1:])]
    wide_kept, *sent = added([kept, across], [rows] * EXPERTS)
    wide_terms = [wide_kept] + [beside(block, "expert", step) for step, block in zip(steps, sent)]
    narrow_kept, sent = added(blocks, [rows] * 2)
    return added_beside([wide_terms, [narrow_kept, beside(sent, "tensor", CORES)]])


def dense(tokens_in, out_grad, expert_ids, gate_probs, w_in, w_out):
    local_rows, features = tokens_in.shape
    together = lax.optimization_barrier
    w_in, w_out = w_in[0], w_out[0]

    grads, both = with_gates(tokens_in, out_grad, expert_ids, gate_probs)
    expert = lax.axis_index("expert").astype(jnp.int32).reshape(1)
    near = beside(both, "expert", NEAR)
    across = beside(both, "tensor", CORES)
    far_tokens = stacked(*[beside(tokens_in, "expert", step) for step in FAR], cost=LONG)
    far_tokens, across, grads, w_in, expert = together((far_tokens, across, grads, w_in, expert))
    near_tokens, near_grads = parted(near, features)
    far_grads = stacked(*[beside(grads, "expert", step) for step in FAR])
    far_tokens_across, near_tokens_across, near_grads_across, far_grads, held_in = together(
        (
            beside(far_tokens, "tensor", CORES),
            beside(near_tokens, "tensor", CORES),
            beside(near_grads, "tensor", CORES),
            far_grads,
            prefetched(w_in, features),
        )
    )
    token_half = stacked(
        both,
        far_tokens,
        near_tokens,
        across,
        far_tokens_across,
        near_tokens_across,
        width=features,
    )
    slope, held_out = slope_rows(
        [token_half, beside(token_half, "tensor", 1)], held_in, w_out, w_out.shape[0]
    )
    grad_column = stacked(
        both, far_grads, near_grads, width=grads.shape[1], offsets=[features, 0, 0]
    )
    far_grads_across, slope, grad_column_other = together(
        (beside(far_grads, "tensor", CORES), slope, beside(grad_column, "tensor", 1))
    )
    grad_across = stacked(
        across, far_grads_across, near_grads_across, width=grads.shape[1], offsets=[features, 0, 0]
    )
    grad_pieces = [grad_column, grad_across, grad_column_other, beside(grad_across, "tensor", 1)]
    count = features * 5 // 8
    scaled, *halves = scaled_rows(
        grad_pieces, expert, held_out, slope, held_in, count
    )
    return scatter_rows(halves, partial_rows(scaled, held_in, count), local_rows)


def local(*args):
    if lax.axis_size("expert") == EXPERTS and lax.axis_size("tensor") == 2 * CORES:
        return dense(*args)
    return routed(*args)


def solution(mesh):
    return jax.shard_map(
        local,
        mesh=mesh,
        in_specs=(
            P(("parts", "expert", "tensor"), None),
            P(("parts", "expert", "tensor"), None),
            P(("parts", "expert", "tensor"), None),
            P(("parts", "expert", "tensor"), None),
            P("expert", None, "tensor"),
            P("expert", "tensor", None),
        ),
        out_specs=P(("parts", "expert", "tensor"), None),
        check_vma=False,
    )
```

```python
import math

import jax
import jax.numpy as jnp
from jax import lax
from jax.experimental import pallas as pl
from jax.experimental.pallas import tpu as pltpu
from jax.sharding import PartitionSpec as P


def gelu_slope(value):
    coeff = math.sqrt(2.0 / math.pi)
    inner = jnp.tanh(coeff * (value + 0.044715 * value * value * value))
    return 0.5 * (1.0 + inner) + 0.5 * value * (1.0 - inner * inner) * coeff * (
        1.0 + 3.0 * 0.044715 * value * value
    )


def slot_table(route_all, experts, capacity):
    flat_ids = route_all.reshape(-1)
    pair_count = flat_ids.shape[0]
    onehot = (flat_ids[:, None] == jnp.arange(experts, dtype=jnp.int32)[None, :]).astype(jnp.int32)
    before = jnp.cumsum(onehot, axis=0) - onehot
    slot_index = jnp.sum(before * onehot, axis=1)
    target = flat_ids * capacity + slot_index
    cell_index = jnp.arange(experts * capacity, dtype=jnp.int32)
    matches = target[None, :] == cell_index[:, None]
    source = jnp.sum(
        jnp.where(matches, jnp.arange(pair_count, dtype=jnp.int32)[None, :], 0), axis=1
    )
    filled = jnp.any(matches, axis=1)
    return (target, source, filled)


def routed(tokens_in, out_grad, expert_ids, gate_probs, w_in, w_out):
    experts = lax.axis_size("expert")
    shards = lax.axis_size("tensor")
    local_rows = tokens_in.shape[0]
    features = tokens_in.shape[1]
    capacity = 3 * local_rows * shards // experts
    route_all = lax.all_gather(expert_ids, "tensor", axis=0, tiled=True)
    target, source, filled = slot_table(route_all, experts, capacity)
    inputs_all, grads_all, gates_all = (
        lax.all_gather(tokens_in, "tensor", axis=0, tiled=True),
        lax.all_gather(out_grad, "tensor", axis=0, tiled=True),
        lax.all_gather(gate_probs, "tensor", axis=0, tiled=True),
    )
    token_of = source // 2
    occupied = filled[:, None]
    send_in = jnp.where(occupied, jnp.take(inputs_all, token_of, axis=0), 0)
    send_in = send_in.reshape(experts, capacity, -1)
    send_grad = jnp.where(occupied, jnp.take(grads_all, token_of, axis=0), 0)
    send_grad = send_grad.reshape(experts, capacity, -1)
    send_gate = jnp.where(filled, jnp.take(gates_all.reshape(-1), source), 0)
    send_gate = send_gate.reshape(experts, capacity)
    rows_in = lax.all_to_all(send_in, "expert", split_axis=0, concat_axis=0, tiled=True)
    rows_grad = lax.all_to_all(send_grad, "expert", split_axis=0, concat_axis=0, tiled=True)
    rows_gate = lax.all_to_all(send_gate, "expert", split_axis=0, concat_axis=0, tiled=True)
    slot_count = rows_in.shape[1]
    flat_in = rows_in.reshape(-1, features)
    flat_grad = rows_grad.reshape(-1, features)
    preact = jnp.dot(flat_in, w_in[0], preferred_element_type=jnp.float32)
    hidden_grad = jnp.einsum("rd,hd->rh", flat_grad, w_out[0], preferred_element_type=jnp.float32)
    scaled = (
        rows_gate.reshape(-1, 1).astype(jnp.float32) * hidden_grad * gelu_slope(preact)
    ).astype(jnp.bfloat16)
    partial_rows = jnp.einsum(
        "rh,dh->rd", scaled, w_in[0], preferred_element_type=jnp.float32
    ).astype(jnp.bfloat16)
    summed = lax.psum(partial_rows, "tensor").astype(jnp.float32)
    outgoing = summed.astype(jnp.bfloat16).reshape(experts, slot_count, -1)
    returned = lax.all_to_all(outgoing, "expert", split_axis=0, concat_axis=0, tiled=True)
    row_table = returned.reshape(experts * capacity, -1)
    offset_row = lax.axis_index("tensor") * (2 * local_rows)
    own_rows = lax.dynamic_slice_in_dim(target, offset_row, 2 * local_rows)
    picked = (
        jnp.take(row_table, own_rows, axis=0).astype(jnp.float32).reshape(local_rows, 2, features)
    )
    return jnp.sum(picked, axis=1).astype(jnp.bfloat16)


CORES = 2
EXPERTS = 4
NEAR, FAR = 1, (3, 2)
LANES = 128
NT = (((1,), (1,)), ((), ()))
VMEM_LIMIT = 10 * 2**20
NO_COST = pl.CostEstimate(flops=0, bytes_accessed=0, transcendentals=0)
LONG = pl.CostEstimate(flops=10**11, bytes_accessed=10**9, transcendentals=0)


def in_vmem(array):
    return pltpu.with_memory_space_constraint(array, pltpu.VMEM)


def whole_block():
    return pl.BlockSpec(memory_space=pltpu.VMEM)


def after(array, *earlier):
    return lax.optimization_barrier((array, *earlier))[0]


def assemble(pieces, rows_ref):
    start = 0
    for piece in pieces:
        rows_ref[pl.ds(start, piece.shape[0]), :] = piece[:, : rows_ref.shape[1]]
        start += piece.shape[0]


def small_kernel(kernel, out_shape, operands, cost=NO_COST):
    return pl.pallas_call(
        kernel,
        out_shape=out_shape,
        in_specs=[whole_block()] * len(operands),
        out_specs=jax.tree.map(lambda _: whole_block(), out_shape),
        compiler_params=pltpu.CompilerParams(vmem_limit_bytes=VMEM_LIMIT),
        cost_estimate=cost,
    )(*operands)


def stacked(*pieces, width=None, offsets=None, cost=NO_COST):
    width = width or pieces[0].shape[1]
    offsets = offsets or [0] * len(pieces)
    rows = sum(piece.shape[0] for piece in pieces)

    def kernel(*refs):
        out_ref = refs[-1]
        start = 0
        for piece, offset in zip(refs, offsets):
            out_ref[pl.ds(start, piece.shape[0]), :] = piece[:, offset : offset + width]
            start += piece.shape[0]

    return small_kernel(kernel, jax.ShapeDtypeStruct((rows, width), jnp.bfloat16), pieces, cost)


def passed(*arrays, cost=NO_COST):
    def kernel(*refs):
        for array_ref, out_ref in zip(refs[: len(arrays)], refs[len(arrays) :]):
            out_ref[...] = array_ref[...]

    out_shape = [jax.ShapeDtypeStruct(array.shape, array.dtype) for array in arrays]
    return small_kernel(kernel, out_shape, arrays, cost)


def parted(array, width, cost=NO_COST):
    def kernel(array_ref, left_ref, right_ref):
        left_ref[...] = array_ref[:, :width]
        right_ref[...] = array_ref[:, width:]

    rows, columns = array.shape
    out_shape = [
        jax.ShapeDtypeStruct((rows, width), jnp.bfloat16),
        jax.ShapeDtypeStruct((rows, columns - width), jnp.bfloat16),
    ]
    return small_kernel(kernel, out_shape, [array], cost)


def added(terms, sizes, sides=1):
    width = terms[0].shape[1]
    half = sum(sizes)

    def kernel(*refs):
        term_refs, out_refs = refs[: len(terms)], refs[len(terms) :]
        start = 0
        for size, out_ref in zip(sizes, out_refs):
            for side in range(sides):
                rows = pl.ds(side * half + start, size)
                total = term_refs[0][rows, :].astype(jnp.float32)
                for term_ref in term_refs[1:]:
                    total += term_ref[rows, :].astype(jnp.float32)
                out_ref[pl.ds(side * size, size), :] = total.astype(jnp.bfloat16)
            start += size

    out_shape = [jax.ShapeDtypeStruct((sides * size, width), jnp.bfloat16) for size in sizes]
    return small_kernel(kernel, out_shape, terms)


def added_beside(chunks):
    rows = chunks[0][0].shape[0]
    widths = [chunk[0].shape[1] for chunk in chunks]
    terms = [term for chunk in chunks for term in chunk]

    def kernel(*refs):
        *term_refs, out_ref = refs
        start = 0
        for chunk, width in zip(chunks, widths):
            group, term_refs = term_refs[: len(chunk)], term_refs[len(chunk) :]
            total = group[0][...].astype(jnp.float32)
            for term_ref in group[1:]:
                total += term_ref[...].astype(jnp.float32)
            out_ref[:, start : start + width] = total.astype(jnp.bfloat16)
            start += width

    return small_kernel(kernel, jax.ShapeDtypeStruct((rows, sum(widths)), jnp.bfloat16), terms)


def in_hbm(array):
    return pltpu.with_memory_space_constraint(array, pltpu.HBM)


def hbm_block():
    return pl.BlockSpec(memory_space=pltpu.HBM)


def with_gates(tokens, grads, expert_ids, gate_probs):
    rows, features = grads.shape

    def kernel(tokens_ref, grads_ref, ids_ref, probs_ref, out_ref, both_ref, ids, probs, sems):
        copies = [
            pltpu.make_async_copy(source, target, sems.at[place])
            for place, (source, target) in enumerate(
                (
                    (ids_ref, ids),
                    (probs_ref, probs),
                    (tokens_ref, both_ref.at[:, pl.ds(0, features)]),
                    (grads_ref, both_ref.at[:, pl.ds(features, features)]),
                    (grads_ref, out_ref.at[:, pl.ds(0, features)]),
                )
            )
        ]
        for copy in copies:
            copy.start()
        copies[0].wait()
        copies[1].wait()
        lane = lax.broadcasted_iota(jnp.int32, (rows, LANES), 1)
        here = lax.broadcasted_iota(jnp.int32, (rows, rows), 0) == lax.broadcasted_iota(
            jnp.int32, (rows, rows), 1
        )
        upright = lambda row: jnp.sum(jnp.where(here, row, 0.0), axis=1, keepdims=True)
        gates = jnp.zeros((rows, LANES), jnp.float32)
        for k in range(ids.shape[0]):
            named = upright(ids[k : k + 1, :].astype(jnp.float32)).astype(jnp.int32)
            prob = upright(probs[k : k + 1, :].astype(jnp.float32))
            gates += jnp.where(lane == named, prob, 0.0)
        out_ref[:, features:] = gates.astype(jnp.bfloat16)
        both_ref[:, 2 * features :] = gates.astype(jnp.bfloat16)
        for copy in copies[2:]:
            copy.wait()

    return pl.pallas_call(
        kernel,
        out_shape=[
            jax.ShapeDtypeStruct((rows, features + LANES), jnp.bfloat16),
            jax.ShapeDtypeStruct((rows, 2 * features + LANES), jnp.bfloat16),
        ],
        in_specs=[hbm_block()] * 4,
        out_specs=[whole_block()] * 2,
        scratch_shapes=[
            pltpu.VMEM(expert_ids.shape[::-1], expert_ids.dtype),
            pltpu.VMEM(gate_probs.shape[::-1], gate_probs.dtype),
            pltpu.SemaphoreType.DMA((5,)),
        ],
        compiler_params=pltpu.CompilerParams(vmem_limit_bytes=VMEM_LIMIT),
        cost_estimate=NO_COST,
    )(in_hbm(tokens), in_hbm(grads), in_hbm(expert_ids.T), in_hbm(gate_probs.T))


def streamed(source_ref, target_ref, sems, first, parts, axis=0):
    size = target_ref.shape[axis] // parts
    copies = []
    for part in range(parts):
        here, there = pl.ds(first + part * size, size), pl.ds(part * size, size)
        if axis == 0:
            ends = source_ref.at[here], target_ref.at[there]
        else:
            ends = source_ref.at[:, here], target_ref.at[:, there]
        copies.append(pltpu.make_async_copy(*ends, sems.at[part]))
        copies[-1].start()
    return copies


def prefetched(weight, rows, parts=2):
    def kernel(weight_ref, out_ref, sems):
        for copy in streamed(weight_ref, out_ref, sems, 0, parts):
            copy.wait()

    return pl.pallas_call(
        kernel,
        out_shape=pltpu.VMEM((rows, weight.shape[1]), weight.dtype),
        in_specs=[hbm_block()],
        out_specs=whole_block(),
        scratch_shapes=[pltpu.SemaphoreType.DMA((parts,))],
        compiler_params=pltpu.CompilerParams(vmem_limit_bytes=VMEM_LIMIT),
        cost_estimate=NO_COST,
    )(in_hbm(weight))


def slope_rows(pieces, weight, later, head, tile=1024):
    rows = sum(piece.shape[0] for piece in pieces)
    features, width = weight.shape

    def kernel(*refs):
        *piece_refs, weight_ref, later_ref, out_ref, head_ref, rows_ref, sems = refs
        copies = streamed(later_ref, head_ref, sems, 0, 1)
        assemble(piece_refs, rows_ref)
        for start in range(0, width, tile):
            cols = pl.ds(start, tile)
            preact = jnp.dot(
                rows_ref[...], weight_ref[:, cols], preferred_element_type=jnp.float32
            )
            out_ref[:, cols] = gelu_slope(preact)
        for copy in copies:
            copy.wait()

    return pl.pallas_call(
        kernel,
        out_shape=[
            jax.ShapeDtypeStruct((rows, width), jnp.float32),
            pltpu.VMEM((head, later.shape[1]), later.dtype),
        ],
        in_specs=[whole_block()] * (len(pieces) + 1) + [hbm_block()],
        out_specs=[whole_block()] * 2,
        scratch_shapes=[
            pltpu.VMEM((rows, features), jnp.bfloat16),
            pltpu.SemaphoreType.DMA((1,)),
        ],
        compiler_params=pltpu.CompilerParams(vmem_limit_bytes=VMEM_LIMIT),
        cost_estimate=NO_COST,
    )(*pieces, in_vmem(weight), in_hbm(later))


def scaled_rows(pieces, expert, weight, slope, back, count, tile=1024):
    rows, width = slope.shape
    features = weight.shape[1]

    def kernel(expert_ref, *refs):
        *piece_refs, weight_ref, slope_ref, back_ref, out_ref, kept_ref, sent_ref = refs[:-2]
        rows_ref, gate_ref = refs[-2:]
        assemble(piece_refs, rows_ref)
        start = 0
        for piece in piece_refs:
            gates = piece[:, features:].astype(jnp.float32)
            lane = lax.broadcasted_iota(jnp.int32, gates.shape, 1)
            gate_ref[pl.ds(start, piece.shape[0]), :] = jnp.sum(
                jnp.where(lane == expert_ref[0], gates, 0.0), axis=1, keepdims=True
            )
            start += piece.shape[0]
        for start in range(0, width, tile):
            cols = pl.ds(start, tile)
            hidden_grad = lax.dot_general(
                rows_ref[...], weight_ref[cols, :], NT, preferred_element_type=jnp.float32
            )
            out_ref[:, cols] = (gate_ref[...] * hidden_grad * slope_ref[:, cols]).astype(
                jnp.bfloat16
            )
        partial_product(out_ref, back_ref, 0, (kept_ref, sent_ref))

    half = jax.ShapeDtypeStruct((rows // CORES, count), jnp.bfloat16)
    return pl.pallas_call(
        kernel,
        out_shape=[jax.ShapeDtypeStruct((rows, width), jnp.bfloat16), half, half],
        in_specs=[pl.BlockSpec(memory_space=pltpu.SMEM)] + [whole_block()] * (len(pieces) + 3),
        out_specs=[whole_block()] * 3,
        scratch_shapes=[
            pltpu.VMEM((rows, features), jnp.bfloat16),
            pltpu.VMEM((rows, 1), jnp.float32),
        ],
        compiler_params=pltpu.CompilerParams(vmem_limit_bytes=VMEM_LIMIT),
        cost_estimate=NO_COST,
    )(expert, *pieces, in_vmem(weight), slope, in_vmem(back))


def partial_product(scaled_ref, weight_ref, first, out_refs):
    half, count = out_refs[0].shape
    product = lax.dot_general(
        scaled_ref[...],
        weight_ref[pl.ds(first, count), :],
        NT,
        preferred_element_type=jnp.float32,
    ).astype(jnp.bfloat16)
    for place, out_ref in enumerate(out_refs):
        out_ref[...] = product[place * half : (place + 1) * half]


def partial_rows(scaled, weight, first):
    rows, count = scaled.shape[0], weight.shape[0] - first

    def kernel(scaled_ref, weight_ref, kept_ref, sent_ref):
        partial_product(scaled_ref, weight_ref, first, (kept_ref, sent_ref))

    half = jax.ShapeDtypeStruct((rows // CORES, count), jnp.bfloat16)
    return pl.pallas_call(
        kernel,
        out_shape=[half, half],
        in_specs=[whole_block()] * 2,
        out_specs=[whole_block()] * 2,
        compiler_params=pltpu.CompilerParams(vmem_limit_bytes=VMEM_LIMIT),
        cost_estimate=NO_COST,
    )(scaled, in_vmem(weight))


def beside(array, axis, step):
    size = lax.axis_size(axis)
    return lax.ppermute(array, axis, [(i, i ^ step) for i in range(size)])


def scatter_rows(wide, narrow, rows):
    steps = (*FAR, NEAR)
    kept, sent = wide
    kept, sent = added([kept, beside(sent, "tensor", 1)], [rows * EXPERTS] * 2)
    across = beside(sent, "tensor", CORES)
    narrow_kept, narrow_sent = narrow
    blocks = added([narrow_kept, beside(narrow_sent, "tensor", 1)], [rows] * EXPERTS, sides=2)
    blocks = [blocks[0]] + [beside(block, "expert", step) for step, block in zip(steps, blocks[1:])]
    wide_kept, *sent = added([kept, across], [rows] * EXPERTS)
    wide_terms = [wide_kept] + [beside(block, "expert", step) for step, block in zip(steps, sent)]
    narrow_kept, sent = added(blocks, [rows] * 2)
    return added_beside([wide_terms, [narrow_kept, beside(sent, "tensor", CORES)]])


def dense(tokens_in, out_grad, expert_ids, gate_probs, w_in, w_out):
    local_rows, features = tokens_in.shape
    together = lax.optimization_barrier
    w_in, w_out = w_in[0], w_out[0]

    grads, both = with_gates(tokens_in, out_grad, expert_ids, gate_probs)
    expert = lax.axis_index("expert").astype(jnp.int32).reshape(1)
    expert, w_in = together((expert, w_in))
    near = beside(both, "expert", NEAR)
    across = beside(both, "tensor", CORES)
    far_tokens = passed(*[beside(tokens_in, "expert", step) for step in FAR], cost=LONG)
    *far_tokens, across, grads, held_in, expert = together(
        (*far_tokens, across, grads, prefetched(w_in, features), expert)
    )
    far_grads = stacked(*[beside(grads, "expert", step) for step in FAR])
    *far_tokens_across, near_across, far_grads = together(
        (
            *[beside(tokens, "tensor", CORES) for tokens in far_tokens],
            beside(near, "tensor", CORES),
            far_grads,
        )
    )
    token_half = stacked(
        both,
        *far_tokens,
        near,
        across,
        *far_tokens_across,
        near_across,
        width=features,
    )
    slope, held_out = slope_rows(
        [token_half, beside(token_half, "tensor", 1)], held_in, w_out, w_out.shape[0]
    )
    grad_column = stacked(
        both, far_grads, near, width=grads.shape[1], offsets=[features, 0, features]
    )
    far_grads_across, slope, grad_column_other = together(
        (beside(far_grads, "tensor", CORES), slope, beside(grad_column, "tensor", 1))
    )
    grad_across = stacked(
        across, far_grads_across, near_across, width=grads.shape[1], offsets=[features, 0, features]
    )
    grad_pieces = [grad_column, grad_across, grad_column_other, beside(grad_across, "tensor", 1)]
    count = features * 5 // 8
    scaled, *halves = scaled_rows(
        grad_pieces, expert, held_out, slope, held_in, count
    )
    return scatter_rows(halves, partial_rows(scaled, held_in, count), local_rows)


def local(*args):
    if lax.axis_size("expert") == EXPERTS and lax.axis_size("tensor") == 2 * CORES:
        return dense(*args)
    return routed(*args)


def solution(mesh):
    return jax.shard_map(
        local,
        mesh=mesh,
        in_specs=(
            P(("parts", "expert", "tensor"), None),
            P(("parts", "expert", "tensor"), None),
            P(("parts", "expert", "tensor"), None),
            P(("parts", "expert", "tensor"), None),
            P("expert", None, "tensor"),
            P("expert", "tensor", None),
        ),
        out_specs=P(("parts", "expert", "tensor"), None),
        check_vma=False,
    )
```

```python
import math

import jax
import jax.numpy as jnp
from jax import lax
from jax.experimental import pallas as pl
from jax.experimental.pallas import tpu as pltpu
from jax.sharding import PartitionSpec as P


def gelu_slope(value):
    coeff = math.sqrt(2.0 / math.pi)
    inner = jnp.tanh(coeff * (value + 0.044715 * value * value * value))
    return 0.5 * (1.0 + inner) + 0.5 * value * (1.0 - inner * inner) * coeff * (
        1.0 + 3.0 * 0.044715 * value * value
    )


def slot_table(route_all, experts, capacity):
    flat_ids = route_all.reshape(-1)
    pair_count = flat_ids.shape[0]
    onehot = (flat_ids[:, None] == jnp.arange(experts, dtype=jnp.int32)[None, :]).astype(jnp.int32)
    before = jnp.cumsum(onehot, axis=0) - onehot
    slot_index = jnp.sum(before * onehot, axis=1)
    target = flat_ids * capacity + slot_index
    cell_index = jnp.arange(experts * capacity, dtype=jnp.int32)
    matches = target[None, :] == cell_index[:, None]
    source = jnp.sum(
        jnp.where(matches, jnp.arange(pair_count, dtype=jnp.int32)[None, :], 0), axis=1
    )
    filled = jnp.any(matches, axis=1)
    return (target, source, filled)


def routed(tokens_in, out_grad, expert_ids, gate_probs, w_in, w_out):
    experts = lax.axis_size("expert")
    shards = lax.axis_size("tensor")
    local_rows = tokens_in.shape[0]
    features = tokens_in.shape[1]
    capacity = 3 * local_rows * shards // experts
    route_all = lax.all_gather(expert_ids, "tensor", axis=0, tiled=True)
    target, source, filled = slot_table(route_all, experts, capacity)
    inputs_all, grads_all, gates_all = (
        lax.all_gather(tokens_in, "tensor", axis=0, tiled=True),
        lax.all_gather(out_grad, "tensor", axis=0, tiled=True),
        lax.all_gather(gate_probs, "tensor", axis=0, tiled=True),
    )
    token_of = source // 2
    occupied = filled[:, None]
    send_in = jnp.where(occupied, jnp.take(inputs_all, token_of, axis=0), 0)
    send_in = send_in.reshape(experts, capacity, -1)
    send_grad = jnp.where(occupied, jnp.take(grads_all, token_of, axis=0), 0)
    send_grad = send_grad.reshape(experts, capacity, -1)
    send_gate = jnp.where(filled, jnp.take(gates_all.reshape(-1), source), 0)
    send_gate = send_gate.reshape(experts, capacity)
    rows_in = lax.all_to_all(send_in, "expert", split_axis=0, concat_axis=0, tiled=True)
    rows_grad = lax.all_to_all(send_grad, "expert", split_axis=0, concat_axis=0, tiled=True)
    rows_gate = lax.all_to_all(send_gate, "expert", split_axis=0, concat_axis=0, tiled=True)
    slot_count = rows_in.shape[1]
    flat_in = rows_in.reshape(-1, features)
    flat_grad = rows_grad.reshape(-1, features)
    preact = jnp.dot(flat_in, w_in[0], preferred_element_type=jnp.float32)
    hidden_grad = jnp.einsum("rd,hd->rh", flat_grad, w_out[0], preferred_element_type=jnp.float32)
    scaled = (
        rows_gate.reshape(-1, 1).astype(jnp.float32) * hidden_grad * gelu_slope(preact)
    ).astype(jnp.bfloat16)
    partial_rows = jnp.einsum(
        "rh,dh->rd", scaled, w_in[0], preferred_element_type=jnp.float32
    ).astype(jnp.bfloat16)
    summed = lax.psum(partial_rows, "tensor").astype(jnp.float32)
    outgoing = summed.astype(jnp.bfloat16).reshape(experts, slot_count, -1)
    returned = lax.all_to_all(outgoing, "expert", split_axis=0, concat_axis=0, tiled=True)
    row_table = returned.reshape(experts * capacity, -1)
    offset_row = lax.axis_index("tensor") * (2 * local_rows)
    own_rows = lax.dynamic_slice_in_dim(target, offset_row, 2 * local_rows)
    picked = (
        jnp.take(row_table, own_rows, axis=0).astype(jnp.float32).reshape(local_rows, 2, features)
    )
    return jnp.sum(picked, axis=1).astype(jnp.bfloat16)


CORES = 2
EXPERTS = 4
NEAR, FAR = 1, (2, 3)
NT = (((1,), (1,)), ((), ()))
VMEM_LIMIT = 10 * 2**20
NO_COST = pl.CostEstimate(flops=0, bytes_accessed=0, transcendentals=0)
LONG = pl.CostEstimate(flops=10**11, bytes_accessed=10**9, transcendentals=0)


def in_vmem(array):
    return pltpu.with_memory_space_constraint(array, pltpu.VMEM)


def whole_block():
    return pl.BlockSpec(memory_space=pltpu.VMEM)


def after(array, *earlier):
    return lax.optimization_barrier((array, *earlier))[0]


def assemble(pieces, rows_ref):
    start = 0
    for piece in pieces:
        rows_ref[pl.ds(start, piece.shape[0]), :] = piece[:, : rows_ref.shape[1]]
        start += piece.shape[0]


def small_kernel(kernel, out_shape, operands, cost=NO_COST):
    return pl.pallas_call(
        kernel,
        out_shape=out_shape,
        in_specs=[whole_block()] * len(operands),
        out_specs=jax.tree.map(lambda _: whole_block(), out_shape),
        compiler_params=pltpu.CompilerParams(vmem_limit_bytes=VMEM_LIMIT),
        cost_estimate=cost,
    )(*operands)


def stacked(*pieces, width=None, offsets=None, cost=NO_COST):
    width = width or pieces[0].shape[1]
    offsets = offsets or [0] * len(pieces)
    rows = sum(piece.shape[0] for piece in pieces)

    def kernel(*refs):
        out_ref = refs[-1]
        start = 0
        for piece, offset in zip(refs, offsets):
            out_ref[pl.ds(start, piece.shape[0]), :] = piece[:, offset : offset + width]
            start += piece.shape[0]

    return small_kernel(kernel, jax.ShapeDtypeStruct((rows, width), jnp.bfloat16), pieces, cost)


def passed(*arrays, cost=NO_COST):
    def kernel(*refs):
        for array_ref, out_ref in zip(refs[: len(arrays)], refs[len(arrays) :]):
            out_ref[...] = array_ref[...]

    out_shape = [jax.ShapeDtypeStruct(array.shape, array.dtype) for array in arrays]
    return small_kernel(kernel, out_shape, arrays, cost)


def added(terms, sizes, sides=1):
    width = terms[0].shape[1]
    half = sum(sizes)

    def kernel(*refs):
        term_refs, out_refs = refs[: len(terms)], refs[len(terms) :]
        start = 0
        for size, out_ref in zip(sizes, out_refs):
            for side in range(sides):
                rows = pl.ds(side * half + start, size)
                total = term_refs[0][rows, :].astype(jnp.float32)
                for term_ref in term_refs[1:]:
                    total += term_ref[rows, :].astype(jnp.float32)
                out_ref[pl.ds(side * size, size), :] = total.astype(jnp.bfloat16)
            start += size

    out_shape = [jax.ShapeDtypeStruct((sides * size, width), jnp.bfloat16) for size in sizes]
    return small_kernel(kernel, out_shape, terms)


def added_beside(chunks):
    rows = chunks[0][0].shape[0]
    widths = [chunk[0].shape[1] for chunk in chunks]
    terms = [term for chunk in chunks for term in chunk]

    def kernel(*refs):
        *term_refs, out_ref = refs
        start = 0
        for chunk, width in zip(chunks, widths):
            group, term_refs = term_refs[: len(chunk)], term_refs[len(chunk) :]
            total = group[0][...].astype(jnp.float32)
            for term_ref in group[1:]:
                total += term_ref[...].astype(jnp.float32)
            out_ref[:, start : start + width] = total.astype(jnp.bfloat16)
            start += width

    return small_kernel(kernel, jax.ShapeDtypeStruct((rows, sum(widths)), jnp.bfloat16), terms)


def in_hbm(array):
    return pltpu.with_memory_space_constraint(array, pltpu.HBM)


def hbm_block():
    return pl.BlockSpec(memory_space=pltpu.HBM)


def gated_rows(tokens, grads, expert_ids, gate_probs, expert):
    rows, features = grads.shape
    steps = (0, NEAR, *FAR)

    def kernel(
        expert_ref, tokens_ref, grads_ref, ids_ref, probs_ref, own_ref, near_ref, *refs
    ):
        far_refs, (held, ids, probs, sems) = refs[: len(FAR)], refs[len(FAR) :]
        copies = [
            pltpu.make_async_copy(source, target, sems.at[place])
            for place, (source, target) in enumerate(
                (
                    (grads_ref, held),
                    (ids_ref, ids),
                    (probs_ref, probs),
                    (tokens_ref, own_ref.at[:, pl.ds(0, features)]),
                    (tokens_ref, near_ref.at[:, pl.ds(0, features)]),
                )
            )
        ]
        for copy in copies:
            copy.start()
        for copy in copies[:3]:
            copy.wait()
        here = lax.broadcasted_iota(jnp.int32, (rows, rows), 0) == lax.broadcasted_iota(
            jnp.int32, (rows, rows), 1
        )
        upright = lambda row: jnp.sum(jnp.where(here, row, 0.0), axis=1, keepdims=True)
        choices = range(ids.shape[0])
        named = [upright(ids[k : k + 1, :].astype(jnp.float32)).astype(jnp.int32) for k in choices]
        chosen = [upright(probs[k : k + 1, :].astype(jnp.float32)) for k in choices]
        rows_grad = held[...].astype(jnp.float32)
        places = (
            own_ref.at[:, pl.ds(features, features)],
            near_ref.at[:, pl.ds(features, features)],
            *far_refs,
        )
        for step, place in zip(steps, places):
            gate = jnp.zeros((rows, 1), jnp.float32)
            for k in choices:
                gate += jnp.where(named[k] == expert_ref[0] ^ step, chosen[k], 0.0)
            place[...] = (gate * rows_grad).astype(jnp.bfloat16)
        for copy in copies[3:]:
            copy.wait()

    wide = jax.ShapeDtypeStruct((rows, 2 * features), jnp.bfloat16)
    return pl.pallas_call(
        kernel,
        out_shape=[wide, wide] + [jax.ShapeDtypeStruct((rows, features), jnp.bfloat16)] * len(FAR),
        in_specs=[pl.BlockSpec(memory_space=pltpu.SMEM)] + [hbm_block()] * 4,
        out_specs=[whole_block()] * (2 + len(FAR)),
        scratch_shapes=[
            pltpu.VMEM((rows, features), jnp.bfloat16),
            pltpu.VMEM(expert_ids.shape[::-1], expert_ids.dtype),
            pltpu.VMEM(gate_probs.shape[::-1], gate_probs.dtype),
            pltpu.SemaphoreType.DMA((5,)),
        ],
        compiler_params=pltpu.CompilerParams(vmem_limit_bytes=VMEM_LIMIT),
        cost_estimate=NO_COST,
    )(expert, in_hbm(tokens), in_hbm(grads), in_hbm(expert_ids.T), in_hbm(gate_probs.T))


def streamed(source_ref, target_ref, sems, first, parts, axis=0):
    size = target_ref.shape[axis] // parts
    copies = []
    for part in range(parts):
        here, there = pl.ds(first + part * size, size), pl.ds(part * size, size)
        if axis == 0:
            ends = source_ref.at[here], target_ref.at[there]
        else:
            ends = source_ref.at[:, here], target_ref.at[:, there]
        copies.append(pltpu.make_async_copy(*ends, sems.at[part]))
        copies[-1].start()
    return copies


def prefetched(weight, rows, parts=2):
    def kernel(weight_ref, out_ref, sems):
        for copy in streamed(weight_ref, out_ref, sems, 0, parts):
            copy.wait()

    return pl.pallas_call(
        kernel,
        out_shape=pltpu.VMEM((rows, weight.shape[1]), weight.dtype),
        in_specs=[hbm_block()],
        out_specs=whole_block(),
        scratch_shapes=[pltpu.SemaphoreType.DMA((parts,))],
        compiler_params=pltpu.CompilerParams(vmem_limit_bytes=VMEM_LIMIT),
        cost_estimate=NO_COST,
    )(in_hbm(weight))


def slope_rows(pieces, weight, later, head, tile=1024):
    rows = sum(piece.shape[0] for piece in pieces)
    features, width = weight.shape

    def kernel(*refs):
        *piece_refs, weight_ref, later_ref, out_ref, head_ref, rows_ref, sems = refs
        copies = streamed(later_ref, head_ref, sems, 0, 1)
        assemble(piece_refs, rows_ref)
        for start in range(0, width, tile):
            cols = pl.ds(start, tile)
            preact = jnp.dot(
                rows_ref[...], weight_ref[:, cols], preferred_element_type=jnp.float32
            )
            out_ref[:, cols] = gelu_slope(preact)
        for copy in copies:
            copy.wait()

    return pl.pallas_call(
        kernel,
        out_shape=[
            jax.ShapeDtypeStruct((rows, width), jnp.float32),
            pltpu.VMEM((head, later.shape[1]), later.dtype),
        ],
        in_specs=[whole_block()] * (len(pieces) + 1) + [hbm_block()],
        out_specs=[whole_block()] * 2,
        scratch_shapes=[
            pltpu.VMEM((rows, features), jnp.bfloat16),
            pltpu.SemaphoreType.DMA((1,)),
        ],
        compiler_params=pltpu.CompilerParams(vmem_limit_bytes=VMEM_LIMIT),
        cost_estimate=NO_COST,
    )(*pieces, in_vmem(weight), in_hbm(later))


def scaled_rows(pieces, weight, slope, back, count, tile=1024):
    rows, width = slope.shape
    features = weight.shape[1]

    def kernel(*refs):
        *piece_refs, weight_ref, slope_ref, back_ref, out_ref, kept_ref, sent_ref, rows_ref = refs
        assemble(piece_refs, rows_ref)
        for start in range(0, width, tile):
            cols = pl.ds(start, tile)
            hidden_grad = lax.dot_general(
                rows_ref[...], weight_ref[cols, :], NT, preferred_element_type=jnp.float32
            )
            out_ref[:, cols] = (hidden_grad * slope_ref[:, cols]).astype(
                jnp.bfloat16
            )
        partial_product(out_ref, back_ref, 0, (kept_ref, sent_ref))

    half = jax.ShapeDtypeStruct((rows // CORES, count), jnp.bfloat16)
    return pl.pallas_call(
        kernel,
        out_shape=[jax.ShapeDtypeStruct((rows, width), jnp.bfloat16), half, half],
        in_specs=[whole_block()] * (len(pieces) + 3),
        out_specs=[whole_block()] * 3,
        scratch_shapes=[
            pltpu.VMEM((rows, features), jnp.bfloat16),
        ],
        compiler_params=pltpu.CompilerParams(vmem_limit_bytes=VMEM_LIMIT),
        cost_estimate=NO_COST,
    )(*pieces, in_vmem(weight), slope, in_vmem(back))


def partial_product(scaled_ref, weight_ref, first, out_refs):
    half, count = out_refs[0].shape
    product = lax.dot_general(
        scaled_ref[...],
        weight_ref[pl.ds(first, count), :],
        NT,
        preferred_element_type=jnp.float32,
    ).astype(jnp.bfloat16)
    for place, out_ref in enumerate(out_refs):
        out_ref[...] = product[place * half : (place + 1) * half]


def partial_rows(scaled, weight, first):
    rows, count = scaled.shape[0], weight.shape[0] - first

    def kernel(scaled_ref, weight_ref, kept_ref, sent_ref):
        partial_product(scaled_ref, weight_ref, first, (kept_ref, sent_ref))

    half = jax.ShapeDtypeStruct((rows // CORES, count), jnp.bfloat16)
    return pl.pallas_call(
        kernel,
        out_shape=[half, half],
        in_specs=[whole_block()] * 2,
        out_specs=[whole_block()] * 2,
        compiler_params=pltpu.CompilerParams(vmem_limit_bytes=VMEM_LIMIT),
        cost_estimate=NO_COST,
    )(scaled, in_vmem(weight))


def beside(array, axis, step):
    size = lax.axis_size(axis)
    return lax.ppermute(array, axis, [(i, i ^ step) for i in range(size)])


def scatter_rows(wide, narrow, rows):
    steps = (*FAR, NEAR)
    kept, sent = wide
    kept, sent = added([kept, beside(sent, "tensor", 1)], [rows * EXPERTS] * 2)
    across = beside(sent, "tensor", CORES)
    narrow_kept, narrow_sent = narrow
    blocks = added([narrow_kept, beside(narrow_sent, "tensor", 1)], [rows] * EXPERTS, sides=2)
    blocks = [blocks[0]] + [beside(block, "expert", step) for step, block in zip(steps, blocks[1:])]
    wide_kept, *sent = added([kept, across], [rows] * EXPERTS)
    wide_terms = [wide_kept] + [beside(block, "expert", step) for step, block in zip(steps, sent)]
    narrow_kept, sent = added(blocks, [rows] * 2)
    return added_beside([wide_terms, [narrow_kept, beside(sent, "tensor", CORES)]])


def dense(tokens_in, out_grad, expert_ids, gate_probs, w_in, w_out):
    local_rows, features = tokens_in.shape
    together = lax.optimization_barrier
    w_in, w_out = w_in[0], w_out[0]

    expert = lax.axis_index("expert").astype(jnp.int32).reshape(1)
    both, both_near, *grads = gated_rows(tokens_in, out_grad, expert_ids, gate_probs, expert)
    near = beside(both_near, "expert", NEAR)
    across = beside(both, "tensor", CORES)
    far_tokens = passed(*[beside(tokens_in, "expert", step) for step in FAR], cost=LONG)
    *values, held_in = together((*far_tokens, across, *grads, prefetched(w_in, features)))
    far_tokens, across, grads = values[: len(FAR)], values[len(FAR)], values[len(FAR) + 1 :]
    far_grads = stacked(*[beside(rows, "expert", step) for rows, step in zip(grads, FAR)])
    *far_tokens_across, near_across, far_grads = together(
        (
            *[beside(tokens, "tensor", CORES) for tokens in far_tokens],
            beside(near, "tensor", CORES),
            far_grads,
        )
    )
    token_half = stacked(
        both,
        *far_tokens,
        near,
        across,
        *far_tokens_across,
        near_across,
        width=features,
    )
    slope, held_out = slope_rows(
        [token_half, beside(token_half, "tensor", 1)], held_in, w_out, w_out.shape[0]
    )
    grad_column = stacked(
        both, far_grads, near, width=features, offsets=[features, 0, features]
    )
    far_grads_across, slope, grad_column_other = together(
        (beside(far_grads, "tensor", CORES), slope, beside(grad_column, "tensor", 1))
    )
    grad_across = stacked(
        across, far_grads_across, near_across, width=features, offsets=[features, 0, features]
    )
    grad_pieces = [grad_column, grad_across, grad_column_other, beside(grad_across, "tensor", 1)]
    count = features * 5 // 8
    scaled, *halves = scaled_rows(
        grad_pieces, held_out, slope, held_in, count
    )
    return scatter_rows(halves, partial_rows(scaled, held_in, count), local_rows)


def local(*args):
    if lax.axis_size("expert") == EXPERTS and lax.axis_size("tensor") == 2 * CORES:
        return dense(*args)
    return routed(*args)


def solution(mesh):
    return jax.shard_map(
        local,
        mesh=mesh,
        in_specs=(
            P(("parts", "expert", "tensor"), None),
            P(("parts", "expert", "tensor"), None),
            P(("parts", "expert", "tensor"), None),
            P(("parts", "expert", "tensor"), None),
            P("expert", None, "tensor"),
            P("expert", "tensor", None),
        ),
        out_specs=P(("parts", "expert", "tensor"), None),
        check_vma=False,
    )
```

```python
import math

import jax
import jax.numpy as jnp
from jax import lax
from jax.experimental import pallas as pl
from jax.experimental.pallas import tpu as pltpu
from jax.sharding import PartitionSpec as P


def gelu_slope(value):
    coeff = math.sqrt(2.0 / math.pi)
    inner = jnp.tanh(coeff * (value + 0.044715 * value * value * value))
    return 0.5 * (1.0 + inner) + 0.5 * value * (1.0 - inner * inner) * coeff * (
        1.0 + 3.0 * 0.044715 * value * value
    )


def slot_table(route_all, experts, capacity):
    flat_ids = route_all.reshape(-1)
    pair_count = flat_ids.shape[0]
    onehot = (flat_ids[:, None] == jnp.arange(experts, dtype=jnp.int32)[None, :]).astype(jnp.int32)
    before = jnp.cumsum(onehot, axis=0) - onehot
    slot_index = jnp.sum(before * onehot, axis=1)
    target = flat_ids * capacity + slot_index
    cell_index = jnp.arange(experts * capacity, dtype=jnp.int32)
    matches = target[None, :] == cell_index[:, None]
    source = jnp.sum(
        jnp.where(matches, jnp.arange(pair_count, dtype=jnp.int32)[None, :], 0), axis=1
    )
    filled = jnp.any(matches, axis=1)
    return (target, source, filled)


def routed(tokens_in, out_grad, expert_ids, gate_probs, w_in, w_out):
    experts = lax.axis_size("expert")
    shards = lax.axis_size("tensor")
    local_rows = tokens_in.shape[0]
    features = tokens_in.shape[1]
    capacity = 3 * local_rows * shards // experts
    route_all = lax.all_gather(expert_ids, "tensor", axis=0, tiled=True)
    target, source, filled = slot_table(route_all, experts, capacity)
    inputs_all, grads_all, gates_all = (
        lax.all_gather(tokens_in, "tensor", axis=0, tiled=True),
        lax.all_gather(out_grad, "tensor", axis=0, tiled=True),
        lax.all_gather(gate_probs, "tensor", axis=0, tiled=True),
    )
    token_of = source // 2
    occupied = filled[:, None]
    send_in = jnp.where(occupied, jnp.take(inputs_all, token_of, axis=0), 0)
    send_in = send_in.reshape(experts, capacity, -1)
    send_grad = jnp.where(occupied, jnp.take(grads_all, token_of, axis=0), 0)
    send_grad = send_grad.reshape(experts, capacity, -1)
    send_gate = jnp.where(filled, jnp.take(gates_all.reshape(-1), source), 0)
    send_gate = send_gate.reshape(experts, capacity)
    rows_in = lax.all_to_all(send_in, "expert", split_axis=0, concat_axis=0, tiled=True)
    rows_grad = lax.all_to_all(send_grad, "expert", split_axis=0, concat_axis=0, tiled=True)
    rows_gate = lax.all_to_all(send_gate, "expert", split_axis=0, concat_axis=0, tiled=True)
    slot_count = rows_in.shape[1]
    flat_in = rows_in.reshape(-1, features)
    flat_grad = rows_grad.reshape(-1, features)
    preact = jnp.dot(flat_in, w_in[0], preferred_element_type=jnp.float32)
    hidden_grad = jnp.einsum("rd,hd->rh", flat_grad, w_out[0], preferred_element_type=jnp.float32)
    scaled = (
        rows_gate.reshape(-1, 1).astype(jnp.float32) * hidden_grad * gelu_slope(preact)
    ).astype(jnp.bfloat16)
    partial_rows = jnp.einsum(
        "rh,dh->rd", scaled, w_in[0], preferred_element_type=jnp.float32
    ).astype(jnp.bfloat16)
    summed = lax.psum(partial_rows, "tensor").astype(jnp.float32)
    outgoing = summed.astype(jnp.bfloat16).reshape(experts, slot_count, -1)
    returned = lax.all_to_all(outgoing, "expert", split_axis=0, concat_axis=0, tiled=True)
    row_table = returned.reshape(experts * capacity, -1)
    offset_row = lax.axis_index("tensor") * (2 * local_rows)
    own_rows = lax.dynamic_slice_in_dim(target, offset_row, 2 * local_rows)
    picked = (
        jnp.take(row_table, own_rows, axis=0).astype(jnp.float32).reshape(local_rows, 2, features)
    )
    return jnp.sum(picked, axis=1).astype(jnp.bfloat16)


CORES = 2
EXPERTS = 4
NEAR, FAR = 1, (2, 3)
NT = (((1,), (1,)), ((), ()))
VMEM_LIMIT = 10 * 2**20
NO_COST = pl.CostEstimate(flops=0, bytes_accessed=0, transcendentals=0)
LONG = pl.CostEstimate(flops=10**11, bytes_accessed=10**9, transcendentals=0)


def in_vmem(array):
    return pltpu.with_memory_space_constraint(array, pltpu.VMEM)


def whole_block():
    return pl.BlockSpec(memory_space=pltpu.VMEM)


def assemble(pieces, rows_ref):
    start = 0
    for piece in pieces:
        rows_ref[pl.ds(start, piece.shape[0]), :] = piece[:, : rows_ref.shape[1]]
        start += piece.shape[0]


def small_kernel(kernel, out_shape, operands, cost=NO_COST):
    return pl.pallas_call(
        kernel,
        out_shape=out_shape,
        in_specs=[whole_block()] * len(operands),
        out_specs=jax.tree.map(lambda _: whole_block(), out_shape),
        compiler_params=pltpu.CompilerParams(vmem_limit_bytes=VMEM_LIMIT),
        cost_estimate=cost,
    )(*operands)


def stacked(*pieces, width=None, offsets=None, cost=NO_COST):
    width = width or pieces[0].shape[1]
    offsets = offsets or [0] * len(pieces)
    rows = sum(piece.shape[0] for piece in pieces)

    def kernel(*refs):
        out_ref = refs[-1]
        start = 0
        for piece, offset in zip(refs, offsets):
            out_ref[pl.ds(start, piece.shape[0]), :] = piece[:, offset : offset + width]
            start += piece.shape[0]

    return small_kernel(kernel, jax.ShapeDtypeStruct((rows, width), jnp.bfloat16), pieces, cost)


def passed(*arrays, cost=NO_COST):
    def kernel(*refs):
        for array_ref, out_ref in zip(refs[: len(arrays)], refs[len(arrays) :]):
            out_ref[...] = array_ref[...]

    out_shape = [jax.ShapeDtypeStruct(array.shape, array.dtype) for array in arrays]
    return small_kernel(kernel, out_shape, arrays, cost)


def added(terms, sizes, sides=1):
    width = terms[0].shape[1]
    half = sum(sizes)

    def kernel(*refs):
        term_refs, out_refs = refs[: len(terms)], refs[len(terms) :]
        start = 0
        for size, out_ref in zip(sizes, out_refs):
            for side in range(sides):
                rows = pl.ds(side * half + start, size)
                total = term_refs[0][rows, :].astype(jnp.float32)
                for term_ref in term_refs[1:]:
                    total += term_ref[rows, :].astype(jnp.float32)
                out_ref[pl.ds(side * size, size), :] = total.astype(jnp.bfloat16)
            start += size

    out_shape = [jax.ShapeDtypeStruct((sides * size, width), jnp.bfloat16) for size in sizes]
    return small_kernel(kernel, out_shape, terms)


def added_beside(chunks):
    rows = chunks[0][0].shape[0]
    widths = [chunk[0].shape[1] for chunk in chunks]
    terms = [term for chunk in chunks for term in chunk]

    def kernel(*refs):
        *term_refs, out_ref = refs
        start = 0
        for chunk, width in zip(chunks, widths):
            group, term_refs = term_refs[: len(chunk)], term_refs[len(chunk) :]
            total = group[0][...].astype(jnp.float32)
            for term_ref in group[1:]:
                total += term_ref[...].astype(jnp.float32)
            out_ref[:, start : start + width] = total.astype(jnp.bfloat16)
            start += width

    return small_kernel(kernel, jax.ShapeDtypeStruct((rows, sum(widths)), jnp.bfloat16), terms)


def in_hbm(array):
    return pltpu.with_memory_space_constraint(array, pltpu.HBM)


def hbm_block():
    return pl.BlockSpec(memory_space=pltpu.HBM)


def gated_rows(tokens, grads, expert_ids, gate_probs, expert):
    rows, features = grads.shape
    steps = (0, NEAR, *FAR)

    def kernel(
        expert_ref, tokens_ref, grads_ref, ids_ref, probs_ref, own_ref, near_ref, *refs
    ):
        far_refs, (held, ids, probs, sems) = refs[: len(FAR)], refs[len(FAR) :]
        copies = [
            pltpu.make_async_copy(source, target, sems.at[place])
            for place, (source, target) in enumerate(
                (
                    (grads_ref, held),
                    (ids_ref, ids),
                    (probs_ref, probs),
                    (tokens_ref, own_ref.at[:, pl.ds(0, features)]),
                    (tokens_ref, near_ref.at[:, pl.ds(0, features)]),
                )
            )
        ]
        for copy in copies:
            copy.start()
        for copy in copies[:3]:
            copy.wait()
        here = lax.broadcasted_iota(jnp.int32, (rows, rows), 0) == lax.broadcasted_iota(
            jnp.int32, (rows, rows), 1
        )
        upright = lambda row: jnp.sum(jnp.where(here, row, 0.0), axis=1, keepdims=True)
        choices = range(ids.shape[0])
        all_ids, all_probs = ids[...].astype(jnp.float32), probs[...].astype(jnp.float32)
        named = [upright(all_ids[k : k + 1]).astype(jnp.int32) for k in choices]
        chosen = [upright(all_probs[k : k + 1]) for k in choices]
        rows_grad = held[...].astype(jnp.float32)
        places = (
            own_ref.at[:, pl.ds(features, features)],
            near_ref.at[:, pl.ds(features, features)],
            *far_refs,
        )
        for step, place in zip(steps, places):
            gate = jnp.zeros((rows, 1), jnp.float32)
            for k in choices:
                gate += jnp.where(named[k] == expert_ref[0] ^ step, chosen[k], 0.0)
            place[...] = (gate * rows_grad).astype(jnp.bfloat16)
        for copy in copies[3:]:
            copy.wait()

    wide = jax.ShapeDtypeStruct((rows, 2 * features), jnp.bfloat16)
    return pl.pallas_call(
        kernel,
        out_shape=[wide, wide] + [jax.ShapeDtypeStruct((rows, features), jnp.bfloat16)] * len(FAR),
        in_specs=[pl.BlockSpec(memory_space=pltpu.SMEM)] + [hbm_block()] * 4,
        out_specs=[whole_block()] * (2 + len(FAR)),
        scratch_shapes=[
            pltpu.VMEM((rows, features), jnp.bfloat16),
            pltpu.VMEM(expert_ids.shape[::-1], expert_ids.dtype),
            pltpu.VMEM(gate_probs.shape[::-1], gate_probs.dtype),
            pltpu.SemaphoreType.DMA((5,)),
        ],
        compiler_params=pltpu.CompilerParams(vmem_limit_bytes=VMEM_LIMIT),
        cost_estimate=NO_COST,
    )(expert, in_hbm(tokens), in_hbm(grads), in_hbm(expert_ids.T), in_hbm(gate_probs.T))


def streamed(source_ref, target_ref, sems, first, parts, axis=0):
    size = target_ref.shape[axis] // parts
    copies = []
    for part in range(parts):
        here, there = pl.ds(first + part * size, size), pl.ds(part * size, size)
        if axis == 0:
            ends = source_ref.at[here], target_ref.at[there]
        else:
            ends = source_ref.at[:, here], target_ref.at[:, there]
        copies.append(pltpu.make_async_copy(*ends, sems.at[part]))
        copies[-1].start()
    return copies


def prefetched(weight, rows, parts=2):
    def kernel(weight_ref, out_ref, sems):
        for copy in streamed(weight_ref, out_ref, sems, 0, parts):
            copy.wait()

    return pl.pallas_call(
        kernel,
        out_shape=pltpu.VMEM((rows, weight.shape[1]), weight.dtype),
        in_specs=[hbm_block()],
        out_specs=whole_block(),
        scratch_shapes=[pltpu.SemaphoreType.DMA((parts,))],
        compiler_params=pltpu.CompilerParams(vmem_limit_bytes=VMEM_LIMIT),
        cost_estimate=NO_COST,
    )(in_hbm(weight))


def slope_rows(pieces, weight, later, head, tile=1024):
    rows = sum(piece.shape[0] for piece in pieces)
    features, width = weight.shape

    def kernel(*refs):
        *piece_refs, weight_ref, later_ref, out_ref, head_ref, rows_ref, sems = refs
        copies = streamed(later_ref, head_ref, sems, 0, 1)
        assemble(piece_refs, rows_ref)
        for start in range(0, width, tile):
            cols = pl.ds(start, tile)
            preact = jnp.dot(
                rows_ref[...], weight_ref[:, cols], preferred_element_type=jnp.float32
            )
            out_ref[:, cols] = gelu_slope(preact)
        for copy in copies:
            copy.wait()

    return pl.pallas_call(
        kernel,
        out_shape=[
            jax.ShapeDtypeStruct((rows, width), jnp.float32),
            pltpu.VMEM((head, later.shape[1]), later.dtype),
        ],
        in_specs=[whole_block()] * (len(pieces) + 1) + [hbm_block()],
        out_specs=[whole_block()] * 2,
        scratch_shapes=[
            pltpu.VMEM((rows, features), jnp.bfloat16),
            pltpu.SemaphoreType.DMA((1,)),
        ],
        compiler_params=pltpu.CompilerParams(vmem_limit_bytes=VMEM_LIMIT),
        cost_estimate=NO_COST,
    )(*pieces, in_vmem(weight), in_hbm(later))


def scaled_rows(pieces, weight, slope, back, count, tile=1024):
    rows, width = slope.shape
    features = weight.shape[1]

    def kernel(*refs):
        *piece_refs, weight_ref, slope_ref, back_ref, out_ref, kept_ref, sent_ref, rows_ref = refs
        assemble(piece_refs, rows_ref)
        for start in range(0, width, tile):
            cols = pl.ds(start, tile)
            hidden_grad = lax.dot_general(
                rows_ref[...], weight_ref[cols, :], NT, preferred_element_type=jnp.float32
            )
            out_ref[:, cols] = (hidden_grad * slope_ref[:, cols]).astype(
                jnp.bfloat16
            )
        partial_product(out_ref, back_ref, 0, (kept_ref, sent_ref))

    half = jax.ShapeDtypeStruct((rows // CORES, count), jnp.bfloat16)
    return pl.pallas_call(
        kernel,
        out_shape=[jax.ShapeDtypeStruct((rows, width), jnp.bfloat16), half, half],
        in_specs=[whole_block()] * (len(pieces) + 3),
        out_specs=[whole_block()] * 3,
        scratch_shapes=[
            pltpu.VMEM((rows, features), jnp.bfloat16),
        ],
        compiler_params=pltpu.CompilerParams(vmem_limit_bytes=VMEM_LIMIT),
        cost_estimate=NO_COST,
    )(*pieces, in_vmem(weight), slope, in_vmem(back))


def partial_product(scaled_ref, weight_ref, first, out_refs):
    half, count = out_refs[0].shape
    product = lax.dot_general(
        scaled_ref[...],
        weight_ref[pl.ds(first, count), :],
        NT,
        preferred_element_type=jnp.float32,
    ).astype(jnp.bfloat16)
    for place, out_ref in enumerate(out_refs):
        out_ref[...] = product[place * half : (place + 1) * half]


def partial_rows(scaled, weight, first):
    rows, count = scaled.shape[0], weight.shape[0] - first

    def kernel(scaled_ref, weight_ref, kept_ref, sent_ref):
        partial_product(scaled_ref, weight_ref, first, (kept_ref, sent_ref))

    half = jax.ShapeDtypeStruct((rows // CORES, count), jnp.bfloat16)
    return pl.pallas_call(
        kernel,
        out_shape=[half, half],
        in_specs=[whole_block()] * 2,
        out_specs=[whole_block()] * 2,
        compiler_params=pltpu.CompilerParams(vmem_limit_bytes=VMEM_LIMIT),
        cost_estimate=NO_COST,
    )(scaled, in_vmem(weight))


def beside(array, axis, step):
    size = lax.axis_size(axis)
    return lax.ppermute(array, axis, [(i, i ^ step) for i in range(size)])


def scatter_rows(wide, narrow, rows):
    steps = (*FAR, NEAR)
    kept, sent = wide
    kept, sent = added([kept, beside(sent, "tensor", 1)], [rows * EXPERTS] * 2)
    across = beside(sent, "tensor", CORES)
    narrow_kept, narrow_sent = narrow
    blocks = added([narrow_kept, beside(narrow_sent, "tensor", 1)], [rows] * EXPERTS, sides=2)
    blocks = [blocks[0]] + [beside(block, "expert", step) for step, block in zip(steps, blocks[1:])]
    wide_kept, *sent = added([kept, across], [rows] * EXPERTS)
    wide_terms = [wide_kept] + [beside(block, "expert", step) for step, block in zip(steps, sent)]
    narrow_kept, sent = added(blocks, [rows] * 2)
    return added_beside([wide_terms, [narrow_kept, beside(sent, "tensor", CORES)]])


def dense(tokens_in, out_grad, expert_ids, gate_probs, w_in, w_out):
    local_rows, features = tokens_in.shape
    together = lax.optimization_barrier
    w_in, w_out = w_in[0], w_out[0]

    expert = lax.axis_index("expert").astype(jnp.int32).reshape(1)
    both, both_near, *grads = gated_rows(tokens_in, out_grad, expert_ids, gate_probs, expert)
    near = beside(both_near, "expert", NEAR)
    across = beside(both, "tensor", CORES)
    far_tokens = passed(*[beside(tokens_in, "expert", step) for step in FAR], cost=LONG)
    *values, held_in = together((*far_tokens, across, *grads, prefetched(w_in, features)))
    far_tokens, across, grads = values[: len(FAR)], values[len(FAR)], values[len(FAR) + 1 :]
    far_grads = stacked(*[beside(rows, "expert", step) for rows, step in zip(grads, FAR)])
    *far_tokens_across, near_across, far_grads = together(
        (
            *[beside(tokens, "tensor", CORES) for tokens in far_tokens],
            beside(near, "tensor", CORES),
            far_grads,
        )
    )
    token_half = stacked(
        both,
        *far_tokens,
        near,
        across,
        *far_tokens_across,
        near_across,
        width=features,
    )
    slope, held_out = slope_rows(
        [token_half, beside(token_half, "tensor", 1)], held_in, w_out, w_out.shape[0]
    )
    grad_column = stacked(
        both, far_grads, near, width=features, offsets=[features, 0, features]
    )
    far_grads_across, slope, grad_column_other = together(
        (beside(far_grads, "tensor", CORES), slope, beside(grad_column, "tensor", 1))
    )
    grad_across = stacked(
        across, far_grads_across, near_across, width=features, offsets=[features, 0, features]
    )
    grad_pieces = [grad_column, grad_across, grad_column_other, beside(grad_across, "tensor", 1)]
    count = features * 5 // 8
    scaled, *halves = scaled_rows(
        grad_pieces, held_out, slope, held_in, count
    )
    return scatter_rows(halves, partial_rows(scaled, held_in, count), local_rows)


def local(*args):
    if lax.axis_size("expert") == EXPERTS and lax.axis_size("tensor") == 2 * CORES:
        return dense(*args)
    return routed(*args)


def solution(mesh):
    return jax.shard_map(
        local,
        mesh=mesh,
        in_specs=(
            P(("parts", "expert", "tensor"), None),
            P(("parts", "expert", "tensor"), None),
            P(("parts", "expert", "tensor"), None),
            P(("parts", "expert", "tensor"), None),
            P("expert", None, "tensor"),
            P("expert", "tensor", None),
        ),
        out_specs=P(("parts", "expert", "tensor"), None),
        check_vma=False,
    )
```

```python
import math

import jax
import jax.numpy as jnp
from jax import lax
from jax.experimental import pallas as pl
from jax.experimental.pallas import tpu as pltpu
from jax.sharding import PartitionSpec as P


def gelu_slope(value):
    coeff = math.sqrt(2.0 / math.pi)
    inner = jnp.tanh(coeff * (value + 0.044715 * value * value * value))
    return 0.5 * (1.0 + inner) + 0.5 * value * (1.0 - inner * inner) * coeff * (
        1.0 + 3.0 * 0.044715 * value * value
    )


def slot_table(route_all, experts, capacity):
    flat_ids = route_all.reshape(-1)
    pair_count = flat_ids.shape[0]
    onehot = (flat_ids[:, None] == jnp.arange(experts, dtype=jnp.int32)[None, :]).astype(jnp.int32)
    before = jnp.cumsum(onehot, axis=0) - onehot
    slot_index = jnp.sum(before * onehot, axis=1)
    target = flat_ids * capacity + slot_index
    cell_index = jnp.arange(experts * capacity, dtype=jnp.int32)
    matches = target[None, :] == cell_index[:, None]
    source = jnp.sum(
        jnp.where(matches, jnp.arange(pair_count, dtype=jnp.int32)[None, :], 0), axis=1
    )
    filled = jnp.any(matches, axis=1)
    return (target, source, filled)


def routed(tokens_in, out_grad, expert_ids, gate_probs, w_in, w_out):
    experts = lax.axis_size("expert")
    shards = lax.axis_size("tensor")
    local_rows = tokens_in.shape[0]
    features = tokens_in.shape[1]
    capacity = 3 * local_rows * shards // experts
    route_all = lax.all_gather(expert_ids, "tensor", axis=0, tiled=True)
    target, source, filled = slot_table(route_all, experts, capacity)
    inputs_all, grads_all, gates_all = (
        lax.all_gather(tokens_in, "tensor", axis=0, tiled=True),
        lax.all_gather(out_grad, "tensor", axis=0, tiled=True),
        lax.all_gather(gate_probs, "tensor", axis=0, tiled=True),
    )
    token_of = source // 2
    occupied = filled[:, None]
    send_in = jnp.where(occupied, jnp.take(inputs_all, token_of, axis=0), 0)
    send_in = send_in.reshape(experts, capacity, -1)
    send_grad = jnp.where(occupied, jnp.take(grads_all, token_of, axis=0), 0)
    send_grad = send_grad.reshape(experts, capacity, -1)
    send_gate = jnp.where(filled, jnp.take(gates_all.reshape(-1), source), 0)
    send_gate = send_gate.reshape(experts, capacity)
    rows_in = lax.all_to_all(send_in, "expert", split_axis=0, concat_axis=0, tiled=True)
    rows_grad = lax.all_to_all(send_grad, "expert", split_axis=0, concat_axis=0, tiled=True)
    rows_gate = lax.all_to_all(send_gate, "expert", split_axis=0, concat_axis=0, tiled=True)
    slot_count = rows_in.shape[1]
    flat_in = rows_in.reshape(-1, features)
    flat_grad = rows_grad.reshape(-1, features)
    preact = jnp.dot(flat_in, w_in[0], preferred_element_type=jnp.float32)
    hidden_grad = jnp.einsum("rd,hd->rh", flat_grad, w_out[0], preferred_element_type=jnp.float32)
    scaled = (
        rows_gate.reshape(-1, 1).astype(jnp.float32) * hidden_grad * gelu_slope(preact)
    ).astype(jnp.bfloat16)
    partial_rows = jnp.einsum(
        "rh,dh->rd", scaled, w_in[0], preferred_element_type=jnp.float32
    ).astype(jnp.bfloat16)
    summed = lax.psum(partial_rows, "tensor").astype(jnp.float32)
    outgoing = summed.astype(jnp.bfloat16).reshape(experts, slot_count, -1)
    returned = lax.all_to_all(outgoing, "expert", split_axis=0, concat_axis=0, tiled=True)
    row_table = returned.reshape(experts * capacity, -1)
    offset_row = lax.axis_index("tensor") * (2 * local_rows)
    own_rows = lax.dynamic_slice_in_dim(target, offset_row, 2 * local_rows)
    picked = (
        jnp.take(row_table, own_rows, axis=0).astype(jnp.float32).reshape(local_rows, 2, features)
    )
    return jnp.sum(picked, axis=1).astype(jnp.bfloat16)


CORES = 2
EXPERTS = 4
NEAR, FAR = 1, (2, 3)
NT = (((1,), (1,)), ((), ()))
VMEM_LIMIT = 10 * 2**20
NO_COST = pl.CostEstimate(flops=0, bytes_accessed=0, transcendentals=0)
LONG = pl.CostEstimate(flops=10**11, bytes_accessed=10**9, transcendentals=0)


def in_vmem(array):
    return pltpu.with_memory_space_constraint(array, pltpu.VMEM)


def whole_block():
    return pl.BlockSpec(memory_space=pltpu.VMEM)


def assemble(pieces, rows_ref):
    start = 0
    for piece in pieces:
        rows_ref[pl.ds(start, piece.shape[0]), :] = piece[:, : rows_ref.shape[1]]
        start += piece.shape[0]


def small_kernel(kernel, out_shape, operands, cost=NO_COST):
    return pl.pallas_call(
        kernel,
        out_shape=out_shape,
        in_specs=[whole_block()] * len(operands),
        out_specs=jax.tree.map(lambda _: whole_block(), out_shape),
        compiler_params=pltpu.CompilerParams(vmem_limit_bytes=VMEM_LIMIT),
        cost_estimate=cost,
    )(*operands)


def stacked(*pieces, width=None, offsets=None, cost=NO_COST):
    width = width or pieces[0].shape[1]
    offsets = offsets or [0] * len(pieces)
    rows = sum(piece.shape[0] for piece in pieces)

    def kernel(*refs):
        out_ref = refs[-1]
        start = 0
        for piece, offset in zip(refs, offsets):
            out_ref[pl.ds(start, piece.shape[0]), :] = piece[:, offset : offset + width]
            start += piece.shape[0]

    return small_kernel(kernel, jax.ShapeDtypeStruct((rows, width), jnp.bfloat16), pieces, cost)


def passed(*arrays, cost=NO_COST):
    def kernel(*refs):
        for array_ref, out_ref in zip(refs[: len(arrays)], refs[len(arrays) :]):
            out_ref[...] = array_ref[...]

    out_shape = [jax.ShapeDtypeStruct(array.shape, array.dtype) for array in arrays]
    return small_kernel(kernel, out_shape, arrays, cost)


def added(terms, sizes, sides=1):
    width = terms[0].shape[1]
    half = sum(sizes)

    def kernel(*refs):
        term_refs, out_refs = refs[: len(terms)], refs[len(terms) :]
        start = 0
        for size, out_ref in zip(sizes, out_refs):
            for side in range(sides):
                rows = pl.ds(side * half + start, size)
                total = term_refs[0][rows, :].astype(jnp.float32)
                for term_ref in term_refs[1:]:
                    total += term_ref[rows, :].astype(jnp.float32)
                out_ref[pl.ds(side * size, size), :] = total.astype(jnp.bfloat16)
            start += size

    out_shape = [jax.ShapeDtypeStruct((sides * size, width), jnp.bfloat16) for size in sizes]
    return small_kernel(kernel, out_shape, terms)


def added_beside(chunks):
    rows = chunks[0][0].shape[0]
    widths = [chunk[0].shape[1] for chunk in chunks]
    terms = [term for chunk in chunks for term in chunk]

    def kernel(*refs):
        *term_refs, out_ref = refs
        start = 0
        for chunk, width in zip(chunks, widths):
            group, term_refs = term_refs[: len(chunk)], term_refs[len(chunk) :]
            total = group[0][...].astype(jnp.float32)
            for term_ref in group[1:]:
                total += term_ref[...].astype(jnp.float32)
            out_ref[:, start : start + width] = total.astype(jnp.bfloat16)
            start += width

    return small_kernel(kernel, jax.ShapeDtypeStruct((rows, sum(widths)), jnp.bfloat16), terms)


def in_hbm(array):
    return pltpu.with_memory_space_constraint(array, pltpu.HBM)


def hbm_block():
    return pl.BlockSpec(memory_space=pltpu.HBM)


def gated_rows(tokens, grads, expert_ids, gate_probs, expert):
    rows, features = grads.shape
    steps = (0, NEAR, *FAR)

    def kernel(
        expert_ref, tokens_ref, grads_ref, ids_ref, probs_ref, own_ref, near_ref, *refs
    ):
        far_refs, (held, ids, probs, sems) = refs[: len(FAR)], refs[len(FAR) :]
        copies = [
            pltpu.make_async_copy(source, target, sems.at[place])
            for place, (source, target) in enumerate(
                (
                    (grads_ref, held),
                    (ids_ref, ids),
                    (probs_ref, probs),
                    (tokens_ref, own_ref.at[:, pl.ds(0, features)]),
                    (tokens_ref, near_ref.at[:, pl.ds(0, features)]),
                )
            )
        ]
        for copy in copies:
            copy.start()
        for copy in copies[:3]:
            copy.wait()
        here = lax.broadcasted_iota(jnp.int32, (rows, rows), 0) == lax.broadcasted_iota(
            jnp.int32, (rows, rows), 1
        )
        upright = lambda row: jnp.sum(jnp.where(here, row, 0.0), axis=1, keepdims=True)
        choices = range(ids.shape[0])
        all_ids, all_probs = ids[...].astype(jnp.float32), probs[...].astype(jnp.float32)
        named = [upright(all_ids[k : k + 1]).astype(jnp.int32) for k in choices]
        chosen = [upright(all_probs[k : k + 1]) for k in choices]
        rows_grad = held[...].astype(jnp.float32)
        places = (
            own_ref.at[:, pl.ds(features, features)],
            near_ref.at[:, pl.ds(features, features)],
            *far_refs,
        )
        for step, place in zip(steps, places):
            gate = jnp.zeros((rows, 1), jnp.float32)
            for k in choices:
                gate += jnp.where(named[k] == expert_ref[0] ^ step, chosen[k], 0.0)
            place[...] = (gate * rows_grad).astype(jnp.bfloat16)
        for copy in copies[3:]:
            copy.wait()

    wide = jax.ShapeDtypeStruct((rows, 2 * features), jnp.bfloat16)
    return pl.pallas_call(
        kernel,
        out_shape=[wide, wide] + [jax.ShapeDtypeStruct((rows, features), jnp.bfloat16)] * len(FAR),
        in_specs=[pl.BlockSpec(memory_space=pltpu.SMEM)] + [hbm_block()] * 4,
        out_specs=[whole_block()] * (2 + len(FAR)),
        scratch_shapes=[
            pltpu.VMEM((rows, features), jnp.bfloat16),
            pltpu.VMEM(expert_ids.shape[::-1], expert_ids.dtype),
            pltpu.VMEM(gate_probs.shape[::-1], gate_probs.dtype),
            pltpu.SemaphoreType.DMA((5,)),
        ],
        compiler_params=pltpu.CompilerParams(vmem_limit_bytes=VMEM_LIMIT),
        cost_estimate=NO_COST,
    )(expert, in_hbm(tokens), in_hbm(grads), in_hbm(expert_ids.T), in_hbm(gate_probs.T))


def streamed(source_ref, target_ref, sems, first, parts, axis=0):
    size = target_ref.shape[axis] // parts
    copies = []
    for part in range(parts):
        here, there = pl.ds(first + part * size, size), pl.ds(part * size, size)
        if axis == 0:
            ends = source_ref.at[here], target_ref.at[there]
        else:
            ends = source_ref.at[:, here], target_ref.at[:, there]
        copies.append(pltpu.make_async_copy(*ends, sems.at[part]))
        copies[-1].start()
    return copies


def prefetched(weight, rows, parts=2):
    def kernel(weight_ref, out_ref, sems):
        for copy in streamed(weight_ref, out_ref, sems, 0, parts):
            copy.wait()

    return pl.pallas_call(
        kernel,
        out_shape=pltpu.VMEM((rows, weight.shape[1]), weight.dtype),
        in_specs=[hbm_block()],
        out_specs=whole_block(),
        scratch_shapes=[pltpu.SemaphoreType.DMA((parts,))],
        compiler_params=pltpu.CompilerParams(vmem_limit_bytes=VMEM_LIMIT),
        cost_estimate=NO_COST,
    )(in_hbm(weight))


def slope_rows(pieces, weight, later, head, tile=1024):
    rows = sum(piece.shape[0] for piece in pieces)
    features, width = weight.shape

    def kernel(*refs):
        *piece_refs, weight_ref, later_ref, out_ref, head_ref, rows_ref, sems = refs
        copies = streamed(later_ref, head_ref, sems, 0, 1)
        assemble(piece_refs, rows_ref)
        for start in range(0, width, tile):
            cols = pl.ds(start, tile)
            preact = jnp.dot(
                rows_ref[...], weight_ref[:, cols], preferred_element_type=jnp.float32
            )
            out_ref[:, cols] = gelu_slope(preact)
        for copy in copies:
            copy.wait()

    return pl.pallas_call(
        kernel,
        out_shape=[
            jax.ShapeDtypeStruct((rows, width), jnp.float32),
            pltpu.VMEM((head, later.shape[1]), later.dtype),
        ],
        in_specs=[whole_block()] * (len(pieces) + 1) + [hbm_block()],
        out_specs=[whole_block()] * 2,
        scratch_shapes=[
            pltpu.VMEM((rows, features), jnp.bfloat16),
            pltpu.SemaphoreType.DMA((1,)),
        ],
        compiler_params=pltpu.CompilerParams(vmem_limit_bytes=VMEM_LIMIT),
        cost_estimate=NO_COST,
    )(*pieces, in_vmem(weight), in_hbm(later))


def scaled_rows(pieces, weight, slope, back, count, tile=2048):
    rows, width = slope.shape
    features = weight.shape[1]

    def kernel(*refs):
        *piece_refs, weight_ref, slope_ref, back_ref, out_ref, kept_ref, sent_ref, rows_ref = refs
        assemble(piece_refs, rows_ref)
        for start in range(0, width, tile):
            cols = pl.ds(start, tile)
            hidden_grad = lax.dot_general(
                rows_ref[...], weight_ref[cols, :], NT, preferred_element_type=jnp.float32
            )
            out_ref[:, cols] = (hidden_grad * slope_ref[:, cols]).astype(
                jnp.bfloat16
            )
        partial_product(out_ref, back_ref, 0, (kept_ref, sent_ref))

    half = jax.ShapeDtypeStruct((rows // CORES, count), jnp.bfloat16)
    return pl.pallas_call(
        kernel,
        out_shape=[jax.ShapeDtypeStruct((rows, width), jnp.bfloat16), half, half],
        in_specs=[whole_block()] * (len(pieces) + 3),
        out_specs=[whole_block()] * 3,
        scratch_shapes=[
            pltpu.VMEM((rows, features), jnp.bfloat16),
        ],
        compiler_params=pltpu.CompilerParams(vmem_limit_bytes=VMEM_LIMIT),
        cost_estimate=NO_COST,
    )(*pieces, in_vmem(weight), slope, in_vmem(back))


def partial_product(scaled_ref, weight_ref, first, out_refs):
    half, count = out_refs[0].shape
    product = lax.dot_general(
        scaled_ref[...],
        weight_ref[pl.ds(first, count), :],
        NT,
        preferred_element_type=jnp.float32,
    ).astype(jnp.bfloat16)
    for place, out_ref in enumerate(out_refs):
        out_ref[...] = product[place * half : (place + 1) * half]


def partial_rows(scaled, weight, first):
    rows, count = scaled.shape[0], weight.shape[0] - first

    def kernel(scaled_ref, weight_ref, kept_ref, sent_ref):
        partial_product(scaled_ref, weight_ref, first, (kept_ref, sent_ref))

    half = jax.ShapeDtypeStruct((rows // CORES, count), jnp.bfloat16)
    return pl.pallas_call(
        kernel,
        out_shape=[half, half],
        in_specs=[whole_block()] * 2,
        out_specs=[whole_block()] * 2,
        compiler_params=pltpu.CompilerParams(vmem_limit_bytes=VMEM_LIMIT),
        cost_estimate=NO_COST,
    )(scaled, in_vmem(weight))


def beside(array, axis, step):
    size = lax.axis_size(axis)
    return lax.ppermute(array, axis, [(i, i ^ step) for i in range(size)])


def scatter_rows(wide, narrow, rows):
    steps = (*FAR, NEAR)
    kept, sent = wide
    kept, sent = added([kept, beside(sent, "tensor", 1)], [rows * EXPERTS] * 2)
    across = beside(sent, "tensor", CORES)
    narrow_kept, narrow_sent = narrow
    blocks = added([narrow_kept, beside(narrow_sent, "tensor", 1)], [rows] * EXPERTS, sides=2)
    blocks = [blocks[0]] + [beside(block, "expert", step) for step, block in zip(steps, blocks[1:])]
    wide_kept, *sent = added([kept, across], [rows] * EXPERTS)
    wide_terms = [wide_kept] + [beside(block, "expert", step) for step, block in zip(steps, sent)]
    narrow_kept, sent = added(blocks, [rows] * 2)
    return added_beside([wide_terms, [narrow_kept, beside(sent, "tensor", CORES)]])


def dense(tokens_in, out_grad, expert_ids, gate_probs, w_in, w_out):
    local_rows, features = tokens_in.shape
    together = lax.optimization_barrier
    w_in, w_out = w_in[0], w_out[0]

    expert = lax.axis_index("expert").astype(jnp.int32).reshape(1)
    both, both_near, *grads = gated_rows(tokens_in, out_grad, expert_ids, gate_probs, expert)
    near = beside(both_near, "expert", NEAR)
    across = beside(both, "tensor", CORES)
    far_tokens = passed(*[beside(tokens_in, "expert", step) for step in FAR], cost=LONG)
    *values, held_in = together((*far_tokens, across, *grads, prefetched(w_in, features)))
    far_tokens, across, grads = values[: len(FAR)], values[len(FAR)], values[len(FAR) + 1 :]
    far_grads = stacked(*[beside(rows, "expert", step) for rows, step in zip(grads, FAR)])
    *far_tokens_across, near_across, far_grads = together(
        (
            *[beside(tokens, "tensor", CORES) for tokens in far_tokens],
            beside(near, "tensor", CORES),
            far_grads,
        )
    )
    token_half = stacked(
        both,
        *far_tokens,
        near,
        across,
        *far_tokens_across,
        near_across,
        width=features,
    )
    slope, held_out = slope_rows(
        [token_half, beside(token_half, "tensor", 1)], held_in, w_out, w_out.shape[0]
    )
    grad_column = stacked(
        both, far_grads, near, width=features, offsets=[features, 0, features]
    )
    far_grads_across, slope, grad_column_other = together(
        (beside(far_grads, "tensor", CORES), slope, beside(grad_column, "tensor", 1))
    )
    grad_across = stacked(
        across, far_grads_across, near_across, width=features, offsets=[features, 0, features]
    )
    grad_pieces = [grad_column, grad_across, grad_column_other, beside(grad_across, "tensor", 1)]
    count = features * 2 // 3
    scaled, *halves = scaled_rows(
        grad_pieces, held_out, slope, held_in, count
    )
    return scatter_rows(halves, partial_rows(scaled, held_in, count), local_rows)


def local(*args):
    if lax.axis_size("expert") == EXPERTS and lax.axis_size("tensor") == 2 * CORES:
        return dense(*args)
    return routed(*args)


def solution(mesh):
    return jax.shard_map(
        local,
        mesh=mesh,
        in_specs=(
            P(("parts", "expert", "tensor"), None),
            P(("parts", "expert", "tensor"), None),
            P(("parts", "expert", "tensor"), None),
            P(("parts", "expert", "tensor"), None),
            P("expert", None, "tensor"),
            P("expert", "tensor", None),
        ),
        out_specs=P(("parts", "expert", "tensor"), None),
        check_vma=False,
    )
```
